32 devices in a mesh: parts: 2 (over y), tile: 4 (over z), ch: 2 (over x), sub: 2 (over core).
Axes of the slice: x: 2, y: 2, z: 4, core: 2. Of those that a mesh axis runs over, the one named last changes fastest.
Arguments:
- feats: bfloat16 [8, 4, 64, 256], P(('parts', 'tile'), ('ch', 'sub')), parts along dimension 0, may hold values from -6 to 6
- weight1: bfloat16 [27, 64, 64], replicated, may hold values from -0.15625 to 0.15625
- bias1: float32 [64], replicated, may hold values from -3 to 3
- weight2: bfloat16 [27, 64, 64], replicated, may hold values from -0.15625 to 0.15625
- bias2: float32 [64], replicated, may hold values from -3 to 3
- cotangent: bfloat16 [8, 4, 64, 256], P(('parts', 'tile'), ('ch', 'sub')), parts along dimension 0, may hold values from -6 to 6
- neighbors: int32 [8, 4, 27, 256], P(('parts', 'tile'), ('ch', 'sub')), parts along dimension 0, may hold values from 0 to 2304, as said below
- shell: int32 [8, 4, 2, 2, 128], P(('parts', 'tile'), ('ch', 'sub')), parts along dimension 0, may hold values from 0 to 256, as said below
Outputs:
- grad_feats: float32 [8, 4, 64, 256], P(('parts', 'tile'), ('ch', 'sub')), parts along dimension 0
- grad_w1: float32 [54, 64, 64], P('parts'), parts along dimension 0
- grad_b1: float32 [128], P('parts'), parts along dimension 0
- grad_w2: float32 [54, 64, 64], P('parts'), parts along dimension 0
- grad_b2: float32 [128], P('parts'), parts along dimension 0
The draws below stay inside these ranges and needn't reach their ends.
There are 2 independent parts, one for each index of `parts`. The reference program is written for one: setup_inputs(seed, part) draws one part's arguments, and reference() takes and returns one part's arrays. A program takes and returns all parts, laid end to end along the dimension named above; an argument that names none is the same for every part. Nothing has to cross between parts.
Inputs may be any that keep to these rules, and one draw needn't show every extreme that they name: Voxels stand in columns of a grid of 32 x 4 * 8 columns, 4 at distinct heights in each; tile (tx, ty) holds the columns of its 8 x 8 square. neighbors[tx, ty, k, v] is the frame row (step frame) of the voxel at v's position plus offset (dx, dy, dz), k = 9 (dx + 1) + 3 (dy + 1) + (dz + 1), or 2304 if that position holds no voxel; if v's offset k points at u, u's offset 26 - k points at v. shell[tx, ty, a, b] lists, in its first (7) * 4 slots, the rows of the tile's voxels in the outermost columns of quadrant (a, b) of its square, 4 for each of 7 columns, each such voxel once; the other slots hold 256.
All inputs are finite; a program needn't handle non-finite values.
Results may differ from the reference program's by a relative error of at most 0.005.
Values may be sent and summed in bfloat16 or wider, within the bound.
A program may use at most 64 MiB of HBM per device.

```python
import math
import jax
import jax.numpy as jnp
import numpy as np
from jax import lax

C = 64
COLS = 8
LEVELS = 4
TX = 4
TY = 4
VOX = 256
HB = 128
SENT = 2304
VOXELS = 4096


def shell_tables():
    half_cols = COLS // 2
    cells = np.zeros((2, 2, (COLS - 1) * LEVELS), np.int32)
    column_slot = np.zeros((COLS, COLS), np.int32)
    for a in range(2):
        for b in range(2):
            edge_x = 0 if a == 0 else COLS - 1
            edge_y = 0 if b == 0 else COLS - 1
            listed = [(edge_x, j) for j in range(b * half_cols, b * half_cols + half_cols)]
            listed = listed + [(i, edge_y) for i in range(a * half_cols, a * half_cols + half_cols) if i != edge_x]
            for position, column in enumerate(listed):
                column_slot[column[0], column[1]] = position
                for j in range(LEVELS):
                    cells[a, b, position * LEVELS + j] = (column[0] * COLS + column[1]) * LEVELS + j
    return (cells, column_slot)


def layout(key):
    key_ground, key_steps, key_order = jax.random.split(key, 3)
    ground = jax.random.randint(key_ground, (COLS * TX, COLS * TY, 1), 0, 4)
    steps_up = jax.random.randint(key_steps, (COLS * TX, COLS * TY, LEVELS), 1, 4)
    heights = ground + jnp.cumsum(steps_up, axis=2)
    scores = jax.random.randint(key_order, (TX, TY, VOX), 0, 65536) * VOX + jnp.arange(VOX, dtype=jnp.int32)
    row_of = jnp.argsort(scores, axis=2).astype(jnp.int32)
    return (heights, row_of)


def draw_shell(key, part):
    heights, row_of = layout(key)
    cells, column_slot = shell_tables()
    picked = row_of[:, :, jnp.asarray(cells)]
    filler = jnp.full((TX, TY, 2, 2, HB - (COLS - 1) * LEVELS), VOX, jnp.int32)
    return jnp.concatenate([picked, filler], axis=4).astype(jnp.int32)


def draw_neighbors(key, part):
    heights, row_of = layout(key)
    cells, column_slot = shell_tables()
    column_slot = jnp.asarray(column_slot)
    width_x = COLS * TX
    width_y = COLS * TY
    glob_x = jnp.arange(width_x, dtype=jnp.int32)[:, None, None]
    glob_y = jnp.arange(width_y, dtype=jnp.int32)[None, :, None]
    level_ids = jnp.arange(LEVELS, dtype=jnp.int32)
    padded = jnp.pad(heights, ((1, 1), (1, 1), (0, 0)), constant_values=-1000)
    results = []
    for shift_x in (-1, 0, 1):
        for shift_y in (-1, 0, 1):
            for shift_z in (-1, 0, 1):
                beside = padded[1 + shift_x:1 + shift_x + width_x, 1 + shift_y:1 + shift_y + width_y, :]
                matches = beside[:, :, None, :] == (heights + shift_z)[:, :, :, None]
                present = jnp.any(matches, axis=3)
                levels_hit = jnp.sum(matches.astype(jnp.int32) * level_ids, axis=3)
                target_x = glob_x + shift_x
                target_y = glob_y + shift_y
                inside = (target_x >= 0) & (target_x < width_x) & (target_y >= 0) & (target_y < width_y)
                clip_x = jnp.clip(target_x, 0, width_x - 1)
                clip_y = jnp.clip(target_y, 0, width_y - 1)
                tile_x = clip_x // COLS
                tile_y = clip_y // COLS
                local_x = clip_x % COLS
                local_y = clip_y % COLS
                tile_dx = tile_x - glob_x // COLS
                tile_dy = tile_y - glob_y // COLS
                cell_index = (local_x * COLS + local_y) * LEVELS + levels_hit
                local_row = row_of[tile_x, tile_y, cell_index]
                upper_x = (local_x >= COLS // 2).astype(jnp.int32)
                upper_y = (local_y >= COLS // 2).astype(jnp.int32)
                block_p = 1 + upper_x + 2 * tile_dx
                block_q = 1 + upper_y + 2 * tile_dy
                halo_row = VOX + (block_p * 4 + block_q) * HB + column_slot[local_x, local_y] * LEVELS + levels_hit
                entry_row = jnp.where((tile_dx == 0) & (tile_dy == 0), local_row, halo_row)
                results.append(jnp.where(present & inside, entry_row, SENT))
    by_cell = jnp.stack(results, axis=0).reshape(27, TX, COLS, TY, COLS, LEVELS)
    by_cell = jnp.transpose(by_cell, (1, 3, 0, 2, 4, 5)).reshape(TX, TY, 27, VOX)
    inverse = jnp.argsort(row_of, axis=2)
    by_row = jnp.take_along_axis(by_cell, inverse[:, :, None, :], axis=3)
    return by_row.astype(jnp.int32)


def level_of(key, extent, cuts, least, largest):
    def one(dim, shards_of):
        draws = jax.random.uniform(jax.random.fold_in(jax.random.fold_in(key, 6), dim), (shards_of,), jnp.float32, least / len(cuts), largest / len(cuts))
        return jnp.repeat(jnp.exp(draws), extent[dim] // shards_of).reshape((-1,) + (1,) * (len(extent) - dim - 1))

    level = one(*cuts[0])
    for cut in cuts[1:]:
        level = level * one(*cut)
    return level


def gaussian(key, shape, scale, reach, shards=(), kind=jnp.bfloat16):
    array = jax.random.normal(key, shape, jnp.float32) * scale
    if len(shards) > 0:
        array = level_of(key, shape, shards, -0.22, 0.18) * array
    return jnp.clip(array, min=-reach, max=reach).astype(kind)


def setup_inputs(seed: int = 0, part: int = 0) -> dict:
    streams_of = jax.random.split(jax.random.key(seed), 9)
    own_keys = jax.random.split(jax.random.fold_in(streams_of[8], part), 9)
    return {
        "feats": gaussian(own_keys[0], (TX, TY, C, VOX), 1.0, 6.0, ((0, 4), (1, 4))),
        "weight1": gaussian(streams_of[1], (27, C, C), (27 * C) ** -0.5, 0.15625),
        "bias1": gaussian(streams_of[2], (C,), 0.5, 3.0, (), jnp.float32),
        "weight2": gaussian(streams_of[3], (27, C, C), (27 * C) ** -0.5, 0.15625),
        "bias2": gaussian(streams_of[4], (C,), 0.5, 3.0, (), jnp.float32),
        "cotangent": gaussian(own_keys[5], (TX, TY, C, VOX), 1.0, 6.0, ((0, 4), (1, 4))),
        "neighbors": draw_neighbors(jax.random.fold_in(jax.random.fold_in(streams_of[8], part), 71), part),
        "shell": draw_shell(jax.random.fold_in(jax.random.fold_in(streams_of[8], part), 71), part),
    }


def silu_slope(values):
    sigmoid = jax.nn.sigmoid(values)
    return sigmoid * (1.0 + values * (1.0 - sigmoid))

def build_frames(source, shell):
    buckets = jax.vmap(jax.vmap(lambda s, i: jnp.take(s, i, axis=1, mode='fill', fill_value=0)))(source, shell)
    bucket_grid = jnp.transpose(buckets, (2, 0, 3, 1, 4, 5)).reshape(C, 2 * TX, 2 * TY, HB)
    bucket_grid = jnp.pad(bucket_grid, ((0, 0), (1, 1), (1, 1), (0, 0)))
    blocks = jnp.stack([jnp.stack([bucket_grid[:, p:p + 2 * TX:2, q:q + 2 * TY:2] for q in range(4)], axis=0) for p in range(4)], axis=0)
    cycle_rows = jnp.transpose(blocks, (3, 4, 2, 0, 1, 5)).reshape(TX * TY, C, 16 * HB)
    return jnp.concatenate([source.reshape(TX * TY, C, VOX), cycle_rows], axis=2)

def convolve(frames, row_table, weight):
    weights = weight.astype(jnp.float32)

    def per_tile(tile_pair):
        framed, near_rows = tile_pair
        running = jnp.zeros((C, VOX), jnp.float32)
        for k in range(3):
            picked = jnp.take(framed, near_rows[9 * k:9 * k + 9], axis=1, mode='fill', fill_value=0).astype(jnp.float32)
            running = running + jnp.einsum('kio,ikr->or', weights[9 * k:9 * k + 9], picked)
        return running
    return lax.map(per_tile, (frames, row_table))

def weight_grad(frames, row_table, gradients):

    def per_tile(running, triple):
        framed, near_rows, gradient = triple
        gradient32 = gradient.astype(jnp.float32)
        pieces = []
        for k in range(3):
            picked = jnp.take(framed, near_rows[9 * k:9 * k + 9], axis=1, mode='fill', fill_value=0).astype(jnp.float32)
            pieces.append(jnp.einsum('ikr,or->kio', picked, gradient32))
        return (running + jnp.concatenate(pieces, axis=0), None)
    total_grad, unused = lax.scan(per_tile, jnp.zeros((27, C, C), jnp.float32), (frames, row_table, gradients))
    return total_grad

def reference(feats, weight1, bias1, weight2, bias2, cotangent, neighbors, shell):
    row_table = neighbors.reshape(TX * TY, 27, VOX)
    flipped = row_table[:, ::-1]
    grad_scale = 1.0 / math.sqrt(VOXELS)
    inputs = feats.reshape(TX * TY, C, VOX)
    frames_in = build_frames(feats, shell)
    first = convolve(frames_in, row_table, weight1) + bias1[None, :, None]
    hidden = jax.nn.silu(first).astype(jnp.bfloat16)
    frames_hidden = build_frames(hidden.reshape(TX, TY, C, VOX), shell)
    second = convolve(frames_hidden, row_table, weight2) + bias2[None, :, None]
    summed = inputs.astype(jnp.float32) + second
    grad_out = (cotangent.reshape(TX * TY, C, VOX).astype(jnp.float32) * silu_slope(summed)).astype(jnp.bfloat16)
    frames_grad = build_frames(grad_out.reshape(TX, TY, C, VOX), shell)
    back_second = convolve(frames_grad, flipped, jnp.swapaxes(weight2, 1, 2))
    grad_pre = (back_second * silu_slope(first)).astype(jnp.bfloat16)
    frames_pre = build_frames(grad_pre.reshape(TX, TY, C, VOX), shell)
    grad_feats = grad_out.astype(jnp.float32) + convolve(frames_pre, flipped, jnp.swapaxes(weight1, 1, 2))
    grad_w2 = weight_grad(frames_hidden, row_table, grad_out) * grad_scale
    grad_b2 = lax.optimization_barrier(jnp.sum(grad_out.astype(jnp.float32), axis=(0, 2))) * grad_scale
    grad_w1 = weight_grad(frames_in, row_table, grad_pre) * grad_scale
    grad_b1 = lax.optimization_barrier(jnp.sum(grad_pre.astype(jnp.float32), axis=(0, 2))) * grad_scale
    return (grad_feats.reshape(TX, TY, C, VOX), grad_w1, grad_b1, grad_w2, grad_b2)
```

```python
import functools
import math

import jax
import jax.numpy as jnp
from jax import lax
from jax.experimental import pallas as pl
from jax.experimental.pallas import tpu as pltpu
from jax.sharding import PartitionSpec as P

BF = jnp.bfloat16
F32 = jnp.float32
MESH = pl.DeviceIdType.MESH
SLOT = 32
PAIRS = 16
OFFS = 27
RING = [(p, q) for p in range(4) for q in range(4) if not (p in (1, 2) and q in (1, 2))]
SHIFT = (-1, 0, 0, 1)
HALF = (1, 0, 1, 0)


def dot(a, b, dims=((1,), (0,))):
    return lax.dot_general(a, b, (dims, ((), ())), preferred_element_type=F32)


def silu_slope(values):
    sigmoid = jax.nn.sigmoid(values)
    return sigmoid * (1.0 + values * (1.0 - sigmoid))


def kernel(
    tiles, chs, subs, scale,
    feats, w1, b1, w2, b2, cot, nbr, shell,
    gf_out, gw1_out, gb1_out, gw2_out, gb2_out,
    onehot, frames, pick_a, pick_b, pick_c, wf1, wf2, wt1, wt2, bucket_sel, buckets, table,
    part, rs1, mid, rs2, full,
    halo_send, halo_recv, s1, r1, s2, r2, s3, r3, s4, r4,
):
    vox = feats.shape[1]
    chan = feats.shape[0]
    tys = chs * subs
    tx = lax.axis_index("tile")
    ty = lax.axis_index("ch") * subs + lax.axis_index("sub")
    quarter = PAIRS * chan // tys
    chunk = max(16, quarter // tiles)
    owners = quarter // chunk
    width = OFFS * chan

    def device(x, y):
        return {"tile": x, "ch": y // subs, "sub": y % subs}

    def exists(dx, dy):
        ok = None
        for at, d, n in ((tx, dx, tiles), (ty, dy, tys)):
            if d:
                here = at > 0 if d < 0 else at < n - 1
                ok = here if ok is None else jnp.logical_and(ok, here)
        return ok

    for stage in range(4):
        frames[stage, vox:, :] = jnp.zeros((16 * SLOT, 2 * chan), BF)

    barrier = pltpu.get_barrier_semaphore()
    for dx in (-1, 0, 1):
        for dy in (-1, 0, 1):
            if dx or dy:

                @pl.when(exists(dx, dy))
                def _():
                    pl.semaphore_signal(
                        barrier, inc=1, device_id=device(tx + dx, ty + dy), device_id_type=MESH
                    )

    for d in range(1, tys):
        pl.semaphore_signal(
            barrier, inc=1, device_id=device(tx, lax.rem(ty + d, tys)), device_id_type=MESH
        )
    for d in range(1, tiles):
        pl.semaphore_signal(
            barrier, inc=1, device_id=device(lax.rem(tx + d, tiles), ty), device_id_type=MESH
        )
    near_x = 1 + jnp.minimum(tx, 1) + jnp.minimum(tiles - 1 - tx, 1)
    near_y = 1 + jnp.minimum(ty, 1) + jnp.minimum(tys - 1 - ty, 1)

    def halo_copy(stage, p, q):
        quad = 2 * HALF[p] + HALF[q]
        return pltpu.make_async_remote_copy(
            src_ref=buckets.at[stage, pl.ds(quad * SLOT, SLOT)],
            dst_ref=frames.at[stage, pl.ds(vox + (4 * p + q) * SLOT, SLOT)],
            send_sem=halo_send.at[stage, 4 * p + q],
            recv_sem=halo_recv.at[stage, 4 * p + q],
            device_id=device(tx - SHIFT[p], ty - SHIFT[q]),
            device_id_type=MESH,
        )

    def send_halo(stage, own):
        frames[stage, :vox, :] = own
        cut = dot(bucket_sel[...], own).astype(BF)
        buckets[stage] = cut
        for p, q in RING:

            @pl.when(exists(-SHIFT[p], -SHIFT[q]))
            def _():
                halo_copy(stage, p, q).start()

        for a in range(2):
            for b in range(2):
                base = vox + (4 * (1 + a) + 1 + b) * SLOT
                quad = 2 * a + b
                frames[stage, base : base + SLOT, :] = cut[quad * SLOT : (quad + 1) * SLOT]

    def wait_halo(stage):
        for p, q in RING:

            @pl.when(exists(SHIFT[p], SHIFT[q]))
            def _():
                halo_copy(stage, p, q).wait_recv()

    def wait_sent(stage):
        for p, q in RING:

            @pl.when(exists(-SHIFT[p], -SHIFT[q]))
            def _():
                halo_copy(stage, p, q).wait_send()

    low = lax.broadcasted_iota(jnp.int32, (vox, 2 * chan), 1) < chan

    def pick(stage, into, flip):
        def pair(j, _):
            k0 = 26 - 2 * j if flip else 2 * j
            k1 = 25 - 2 * j if flip else 2 * j + 1
            framed = frames[stage]
            first = dot(onehot[k0], framed)
            second = dot(onehot[k1], framed)
            at = pl.multiple_of(j * 2 * chan, 2 * chan)
            into[:, pl.ds(at, 2 * chan)] = jnp.where(low, first, second).astype(BF)
            return 0

        lax.fori_loop(0, OFFS // 2, pair, 0)
        last = dot(onehot[0 if flip else 26], frames[stage])
        into[:, width - chan :] = jnp.where(low, last, 1.0).astype(BF)

    quads = [shell[a, b : b + 1, :][:, :SLOT] for a in range(2) for b in range(2)]
    listed = jnp.concatenate(quads, axis=1)
    by_voxel = lax.broadcasted_iota(jnp.int32, (vox, 4 * SLOT), 0) == listed
    bucket_sel[...] = jnp.where(by_voxel, 1.0, 0.0).T.astype(BF)

    both = feats[...].astype(F32)
    inputs = jnp.concatenate([both, both], axis=0).T
    pl.semaphore_wait(barrier, near_x * near_y - 1 + (tys - 1) + (tiles - 1))
    send_halo(0, inputs.astype(BF))

    index = nbr[...]
    outer = index - vox
    slot = jnp.bitwise_and(outer, 127)
    packed = vox + lax.shift_right_logical(outer, 7) * SLOT + slot
    known = jnp.logical_and(index < vox + 16 * 128, slot < SLOT)
    packed = jnp.where(index < vox, index, jnp.where(known, packed, -1))
    table[...] = jnp.concatenate(
        [packed, jnp.zeros((128 - OFFS, vox), jnp.int32)], axis=0
    ).T
    columns = vox + 16 * SLOT
    block = 32

    def build(i, _):
        rows = pl.ds(pl.multiple_of(i * block, block), block)
        entries = table[rows, :]
        lanes = lax.broadcasted_iota(jnp.int32, (block, columns), 1)
        for k in range(OFFS):
            hit = entries[:, k : k + 1] == lanes
            onehot[k, rows, :] = jnp.where(hit, 1.0, 0.0).astype(BF)
        return 0

    lax.fori_loop(0, vox // block, build, 0)

    for weight, forward, turned in ((w1, wf1, wt1), (w2, wf2, wt2)):
        for k in range(OFFS):
            value = weight[k]
            forward[k * chan : (k + 1) * chan, :] = jnp.concatenate([value, value], axis=1)
        forward[width:, :] = jnp.zeros((chan, 2 * chan), BF)
        for j in range(PAIRS - 2):
            left = weight[2 * j]
            right = weight[2 * j + 1] if 2 * j + 1 < OFFS else jnp.zeros((chan, chan), BF)
            beside = jnp.concatenate([left, right], axis=1)
            turned[:chan, 2 * chan * j : 2 * chan * (j + 1)] = beside
            turned[chan:, 2 * chan * j : 2 * chan * (j + 1)] = beside

    def twice(bias):
        return jnp.concatenate([bias[...], bias[...]], axis=1)

    def ty_copy(g, d):
        to = lax.rem(ty + d, tys)
        return pltpu.make_async_remote_copy(
            src_ref=part.at[g, pl.ds(pl.multiple_of(to * quarter, quarter), quarter)],
            dst_ref=rs1.at[g, d],
            send_sem=s1.at[g, d],
            recv_sem=r1.at[g, d],
            device_id=device(tx, to),
            device_id_type=MESH,
        )

    def tile_copy(g, d):
        to = lax.rem(tx + d, tiles)
        at = pl.multiple_of(lax.rem(to, owners) * chunk, chunk)
        return pltpu.make_async_remote_copy(
            src_ref=mid.at[g, pl.ds(at, chunk)],
            dst_ref=rs2.at[g, d],
            send_sem=s2.at[g, d],
            recv_sem=r2.at[g, d],
            device_id=device(to, ty),
            device_id_type=MESH,
        )

    def chunk_rows(x):
        return pl.ds(pl.multiple_of(ty * quarter + lax.rem(x, owners) * chunk, chunk), chunk)

    def back_tile(g, d, x):
        return pltpu.make_async_remote_copy(
            src_ref=full.at[g, chunk_rows(x)],
            dst_ref=full.at[g, chunk_rows(x)],
            send_sem=s3.at[g, d],
            recv_sem=r3.at[g, d],
            device_id=device(lax.rem(tx + d, tiles), ty),
            device_id_type=MESH,
        )

    def back_ty(g, d, y):
        rows = pl.ds(pl.multiple_of(y * quarter, quarter), quarter)
        return pltpu.make_async_remote_copy(
            src_ref=full.at[g, rows],
            dst_ref=full.at[g, rows],
            send_sem=s4.at[g, d],
            recv_sem=r4.at[g, d],
            device_id=device(tx, lax.rem(ty + d, tys)),
            device_id_type=MESH,
        )

    def owned(x, body):
        if owners >= tiles:
            body()
        else:
            pl.when(x < owners)(body)

    def reduce_start(g, gradient, picked):
        turned = gradient.T[:chan].astype(BF)
        terms = dot(turned, picked[...])
        for j in range(PAIRS - 2):
            part[g, j * chan : (j + 1) * chan, :] = terms[
                :, 2 * chan * j : 2 * chan * (j + 1)
            ].astype(BF)
        part[g, (PAIRS - 2) * chan :, :] = jnp.zeros((2 * chan, 2 * chan), BF)
        for d in range(1, tys):
            ty_copy(g, d).start()

    def reduce_tiles(g):
        for d in range(1, tys):
            ty_copy(g, d).wait_recv()
        own = pl.ds(pl.multiple_of(ty * quarter, quarter), quarter)
        total = part[g, own, :].astype(F32)
        for d in range(1, tys):
            total = total + rs1[g, d].astype(F32)
        for j in range(quarter // chan):
            flat = total[j * chan : (j + 1) * chan].T
            mid[g, j * chan : (j + 1) * chan, :] = jnp.concatenate(
                [flat[:chan], flat[chan:]], axis=1
            ).astype(BF)
        for d in range(1, tiles):
            owned(lax.rem(tx + d, tiles), lambda: tile_copy(g, d).start())

    def spread_tiles(g):
        def body():
            for d in range(1, tiles):
                tile_copy(g, d).wait_recv()
            at = pl.multiple_of(lax.rem(tx, owners) * chunk, chunk)
            total = mid[g, pl.ds(at, chunk), :].astype(F32)
            for d in range(1, tiles):
                total = total + rs2[g, d].astype(F32)
            full[g, chunk_rows(tx), :] = total.astype(BF)
            for d in range(1, tiles):
                back_tile(g, d, tx).start()

        owned(tx, body)

    def spread_ty(g):
        for d in range(1, tiles):
            source = lax.rem(tx - d + tiles, tiles)
            owned(source, lambda: back_tile(g, d, source).wait_recv())
        for d in range(1, tys):
            back_ty(g, d, ty).start()

    def finish(g, gw_out, gb_out):
        for d in range(1, tys):
            back_ty(g, d, lax.rem(ty - d + tys, tys)).wait_recv()
        for j in range(PAIRS - 2):
            value = full[g, j * chan : (j + 1) * chan, :].astype(F32) * scale
            gw_out[2 * j] = value[:, :chan]
            if 2 * j + 1 < OFFS:
                gw_out[2 * j + 1] = value[:, chan:]
            else:
                gb_out[...] = value[:1, chan:]

    def drain(g):
        for d in range(1, tys):
            ty_copy(g, d).wait_send()
            back_ty(g, d, ty).wait_send()
        for d in range(1, tiles):
            owned(lax.rem(tx + d, tiles), lambda: tile_copy(g, d).wait_send())
            owned(tx, lambda: back_tile(g, d, tx).wait_send())

    wait_halo(0)
    pick(0, pick_a, False)
    first = dot(pick_a[...], wf1[...]) + twice(b1)
    hidden = (first * jax.nn.sigmoid(first)).astype(BF)
    send_halo(1, hidden)
    upstream = cot[...].astype(F32)
    upstream = jnp.concatenate([upstream, upstream], axis=0).T
    wait_halo(1)
    pick(1, pick_b, False)
    second = dot(pick_b[...], wf2[...]) + twice(b2)
    grad_out = (upstream * silu_slope(inputs + second)).astype(BF)

    send_halo(2, grad_out)
    grad_out = grad_out.astype(F32)
    reduce_start(1, grad_out, pick_b)
    wait_halo(2)
    pick(2, pick_c, True)
    back = dot(pick_c[...], wt2[...], ((1,), (1,)))
    grad_pre = (back * silu_slope(first)).astype(BF)
    send_halo(3, grad_pre)
    reduce_start(0, grad_pre.astype(F32), pick_a)
    reduce_tiles(1)
    wait_halo(3)
    pick(3, pick_c, True)
    reduce_tiles(0)
    spread_tiles(1)
    back = dot(pick_c[...], wt1[...], ((1,), (1,)))
    gf_out[...] = (grad_out + back).T[:chan]
    spread_tiles(0)
    spread_ty(1)
    spread_ty(0)
    finish(1, gw2_out, gb2_out)
    finish(0, gw1_out, gb1_out)
    for stage in range(4):
        wait_sent(stage)
    drain(1)
    drain(0)


def per_device(feats, weight1, bias1, weight2, bias2, cotangent, neighbors, shell):
    tiles, chs, subs = (lax.axis_size(a) for a in ("tile", "ch", "sub"))
    chan, vox = feats.shape[2:]
    tys = chs * subs
    scale = 1.0 / math.sqrt(vox * tiles * tys)
    columns = vox + 16 * SLOT
    rows = PAIRS * chan
    quarter = rows // tys
    chunk = max(16, quarter // tiles)
    wide = (PAIRS - 2) * 2 * chan
    lanes = 2 * chan
    vmem = pl.BlockSpec(memory_space=pltpu.VMEM)
    dma = pltpu.SemaphoreType.DMA
    gf, gw1, gb1, gw2, gb2 = pl.pallas_call(
        functools.partial(kernel, tiles, chs, subs, scale),
        out_shape=(
            jax.ShapeDtypeStruct((chan, vox), F32),
            jax.ShapeDtypeStruct((OFFS, chan, chan), F32),
            jax.ShapeDtypeStruct((1, chan), F32),
            jax.ShapeDtypeStruct((OFFS, chan, chan), F32),
            jax.ShapeDtypeStruct((1, chan), F32),
        ),
        in_specs=[vmem] * 8,
        out_specs=(vmem,) * 5,
        scratch_shapes=[
            pltpu.VMEM((OFFS, vox, columns), BF),
            pltpu.VMEM((4, columns, lanes), BF),
            pltpu.VMEM((vox, wide), BF),
            pltpu.VMEM((vox, wide), BF),
            pltpu.VMEM((vox, wide), BF),
            pltpu.VMEM((wide, lanes), BF),
            pltpu.VMEM((wide, lanes), BF),
            pltpu.VMEM((lanes, wide), BF),
            pltpu.VMEM((lanes, wide), BF),
            pltpu.VMEM((4 * SLOT, vox), BF),
            pltpu.VMEM((4, 4 * SLOT, lanes), BF),
            pltpu.VMEM((vox, 128), jnp.int32),
            pltpu.VMEM((2, rows, lanes), BF),
            pltpu.VMEM((2, tys, quarter, lanes), BF),
            pltpu.VMEM((2, quarter, lanes), BF),
            pltpu.VMEM((2, tiles, chunk, lanes), BF),
            pltpu.VMEM((2, rows, lanes), BF),
            dma((4, 16)),
            dma((4, 16)),
            dma((2, tys)),
            dma((2, tys)),
            dma((2, tiles)),
            dma((2, tiles)),
            dma((2, tiles)),
            dma((2, tiles)),
            dma((2, tys)),
            dma((2, tys)),
        ],
        compiler_params=pltpu.CompilerParams(
            collective_id=0, has_side_effects=True, vmem_limit_bytes=48 * 1024 * 1024
        ),
    )(
        feats[0, 0], weight1, bias1[None], weight2, bias2[None], cotangent[0, 0],
        neighbors[0, 0], shell[0, 0],
    )
    return gf[None, None], gw1, gb1[0], gw2, gb2[0]


def solution(mesh):
    placed = (
        P(("parts", "tile"), ("ch", "sub"), None, None),
        P(),
        P(),
        P(),
        P(),
        P(("parts", "tile"), ("ch", "sub"), None, None),
        P(("parts", "tile"), ("ch", "sub"), None, None),
        P(("parts", "tile"), ("ch", "sub"), None, None, None),
    )
    return jax.shard_map(
        per_device,
        mesh=mesh,
        in_specs=placed,
        out_specs=(
            P(("parts", "tile"), ("ch", "sub"), None, None),
            P("parts", None, None),
            P("parts"),
            P("parts", None, None),
            P("parts"),
        ),
        check_vma=False,
    )
```

```python
import functools
import math

import jax
import jax.numpy as jnp
from jax import lax
from jax.experimental import pallas as pl
from jax.experimental.pallas import tpu as pltpu
from jax.sharding import PartitionSpec as P

BF = jnp.bfloat16
F32 = jnp.float32
MESH = pl.DeviceIdType.MESH
SLOT = 32
PAIRS = 16
OFFS = 27
UNROLL = 7
RING = [
    (0, 0), (0, 1), (0, 2), (0, 3), (1, 3), (2, 3),
    (3, 3), (3, 2), (3, 1), (3, 0), (2, 0), (1, 0),
]
BESIDE = 5
FIRST = (10, 1, 7, 4)
SHIFT = (-1, 0, 0, 1)
HALF = (1, 0, 1, 0)


def dot(a, b, dims=((1,), (0,))):
    return lax.dot_general(a, b, (dims, ((), ())), preferred_element_type=F32)


def silu_slope(values):
    sigmoid = jax.nn.sigmoid(values)
    return sigmoid * (1.0 + values * (1.0 - sigmoid))


def kernel(
    tiles, chs, subs,
    feats_in, w1_in, b1, w2_in, b2, cot_in, nbr_in, shell_in,
    gf_out, full_out,
    feats, w1, w2, cot, nbr, shell, in_sem,
    own_hot, halo_hot, ring, own_a, own_b, own_c, halo_a, halo_b, halo_c,
    wf1, wf2, wt1, wt2, gather_sel, scatter_sel, buckets, table,
    part, rs1, mid, rs2, full,
    halo_send, halo_recv, s1, r1, s2, r2, s3, r3, s4, r4,
):
    vox = feats.shape[1]
    chan = feats.shape[0]
    lanes = 2 * chan
    width = OFFS * chan
    tys = chs * subs
    tx = lax.axis_index("tile")
    ty = lax.axis_index("ch") * subs + lax.axis_index("sub")
    quarter = PAIRS * chan // tys
    chunk = max(chan, quarter // tiles)
    owners = quarter // chunk

    loads = [
        pltpu.make_async_copy(src, dst, in_sem.at[i])
        for i, (src, dst) in enumerate((
            (feats_in.at[0, 0], feats),
            (shell_in.at[0, 0], shell),
            (nbr_in.at[0, 0], nbr),
            (w1_in, w1),
            (cot_in.at[0, 0], cot),
            (w2_in, w2),
        ))
    ]
    for load in loads:
        load.start()

    def device(x, y):
        return {"tile": x, "ch": y // subs, "sub": y % subs}

    def exists(dx, dy):
        ok = None
        for at, d, n in ((tx, dx, tiles), (ty, dy, tys)):
            if d:
                here = at > 0 if d < 0 else at < n - 1
                ok = here if ok is None else jnp.logical_and(ok, here)
        return ok

    for stage in range(4):
        ring[stage] = jnp.zeros(ring.shape[1:], BF)

    barrier = pltpu.get_barrier_semaphore()
    for dx in (-1, 0, 1):
        for dy in (-1, 0, 1):
            if dx or dy:

                @pl.when(exists(dx, dy))
                def _():
                    pl.semaphore_signal(
                        barrier, inc=1, device_id=device(tx + dx, ty + dy), device_id_type=MESH
                    )

    for d in range(1, tys):
        pl.semaphore_signal(
            barrier, inc=1, device_id=device(tx, lax.rem(ty + d, tys)), device_id_type=MESH
        )
    for d in range(1, tiles):
        pl.semaphore_signal(
            barrier, inc=1, device_id=device(lax.rem(tx + d, tiles), ty), device_id_type=MESH
        )
    near_x = 1 + jnp.minimum(tx, 1) + jnp.minimum(tiles - 1 - tx, 1)
    near_y = 1 + jnp.minimum(ty, 1) + jnp.minimum(tys - 1 - ty, 1)

    def halo_copy(stage, n):
        p, q = RING[n]
        quad = 2 * HALF[p] + HALF[q]
        return pltpu.make_async_remote_copy(
            src_ref=buckets.at[stage, pl.ds(quad * SLOT, SLOT)],
            dst_ref=ring.at[stage, pl.ds(n * SLOT, SLOT)],
            send_sem=halo_send.at[stage, n],
            recv_sem=halo_recv.at[stage, n],
            device_id=device(tx - SHIFT[p], ty - SHIFT[q]),
            device_id_type=MESH,
        )

    def outgoing(n):
        return exists(-SHIFT[RING[n][0]], -SHIFT[RING[n][1]])

    def incoming(n):
        return exists(SHIFT[RING[n][0]], SHIFT[RING[n][1]])

    def send_halo(stage, own):
        buckets[stage] = dot(gather_sel[...], own).astype(BF)
        for n in range(len(RING)):

            @pl.when(outgoing(n))
            def _():
                halo_copy(stage, n).start()

    def wait_halo(stage):
        for n in range(len(RING)):

            @pl.when(incoming(n))
            def _():
                halo_copy(stage, n).wait_recv()

        again = ring.shape[1] - len(RING) * SLOT
        ring[stage, len(RING) * SLOT :, :] = ring[stage, :again, :]

    def wait_sent(stage):
        for n in range(len(RING)):

            @pl.when(outgoing(n))
            def _():
                halo_copy(stage, n).wait_send()

    def pick_own(own, into, flip):
        low = lax.broadcasted_iota(jnp.int32, (vox, lanes), 1) < chan
        step = UNROLL

        def some(i, _):
            for u in range(step):
                j = i * step + u
                first = (OFFS - 1) - 2 * j if flip else 2 * j + 1
                rows = pl.ds(pl.multiple_of(first * vox, vox), 2 * vox)
                both = dot(own_hot[rows, :], own)
                ahead, behind = both[:vox], both[vox:]
                if flip:
                    ahead, behind = behind, ahead
                at = pl.multiple_of(j * lanes, lanes)
                into[:, pl.ds(at, lanes)] = jnp.where(low, ahead, behind).astype(BF)
            return 0

        lax.fori_loop(0, (PAIRS - 2) // step, some, 0)
        last = into[:, width - chan :]
        into[:, width - chan :] = jnp.where(low, last, jnp.ones_like(last))

    def pick_halo(stage, into, flip):
        low = lax.broadcasted_iota(jnp.int32, (SLOT, lanes), 1) < chan
        for quad in range(4):
            near = ring[stage, FIRST[quad] * SLOT : (FIRST[quad] + BESIDE) * SLOT, :]
            found = dot(halo_hot[quad], near)
            for j in range(PAIRS - 2):
                k0, k1 = (OFFS - 2 * j, OFFS - 1 - 2 * j) if flip else (2 * j + 1, 2 * j + 2)
                into[quad * SLOT : (quad + 1) * SLOT, j * lanes : (j + 1) * lanes] = jnp.where(
                    low, found[k0 * SLOT : (k0 + 1) * SLOT], found[k1 * SLOT : (k1 + 1) * SLOT]
                ).astype(BF)

    def convolve(own_picked, halo_picked, weight, dims):
        edge = dot(halo_picked[...], weight[...], dims)
        high = edge.astype(BF)
        low = (edge - high.astype(F32)).astype(BF)
        inner = dot(own_picked[...], weight[...], dims)
        return inner + dot(scatter_sel[...], jnp.concatenate([high, low], axis=0))

    loads[0].wait()
    loads[1].wait()
    quads = [shell[a, b : b + 1, :][:, :SLOT] for a in range(2) for b in range(2)]
    listed = jnp.concatenate(quads, axis=1)
    by_voxel = lax.broadcasted_iota(jnp.int32, (vox, 4 * SLOT), 0) == listed
    scatter = jnp.where(by_voxel, 1.0, 0.0)
    gather = scatter.T
    gather_sel[...] = gather.astype(BF)
    scatter_sel[...] = jnp.concatenate([scatter, scatter], axis=1).astype(BF)

    both = feats[...].astype(F32)
    inputs = jnp.concatenate([both, both], axis=0).T
    pl.semaphore_wait(barrier, near_x * near_y - 1 + (tys - 1) + (tiles - 1))
    send_halo(0, inputs.astype(BF))

    loads[2].wait()
    index = nbr[...]
    outer = index - vox
    slot = jnp.bitwise_and(outer, 127)
    block = lax.shift_right_logical(outer, 7)
    position = jnp.full(index.shape, 15, jnp.int32)
    for n, (p, q) in enumerate(RING):
        position = jnp.where(block == 4 * p + q, n, position)
    position = jnp.where(jnp.logical_and(index >= vox, slot < SLOT), position, 15)
    slot = jnp.bitwise_and(slot, SLOT - 1)
    fill = jnp.zeros((32 - OFFS, vox), F32)
    stacked = [position.astype(F32), fill, slot.astype(F32), fill, index.astype(F32), fill]
    stacked = jnp.concatenate(stacked + [jnp.zeros((32, vox), F32)], axis=0).T
    table[...] = stacked

    place = lax.broadcasted_iota(jnp.int32, (4 * SLOT, vox), 0)
    quad_of = lax.shift_right_logical(place, 5)
    frame_block = 5 + 4 * lax.shift_right_logical(quad_of, 1) + jnp.bitwise_and(quad_of, 1)
    frame_row = vox + 128 * frame_block + jnp.bitwise_and(place, SLOT - 1)
    alias = jnp.where(gather > 0.5, frame_row.astype(F32), -1.0)
    alias = jnp.max(alias, axis=0, keepdims=True)
    own_hot[:vox, :] = jnp.zeros((vox, vox), BF)
    own_hot[(OFFS + 1) * vox :, :] = jnp.zeros((vox, vox), BF)
    height = 32

    def build(i, _):
        base = i * height
        entries = table[pl.ds(pl.multiple_of(base, height), height), :]
        row = lax.broadcasted_iota(jnp.int32, (height, vox), 1).astype(F32)
        for k in range(OFFS):
            entry = entries[:, 64 + k : 65 + k]
            hit = jnp.logical_or(entry == row, entry == alias)
            at = pl.multiple_of((k + 1) * vox + base, height)
            own_hot[pl.ds(at, height), :] = jnp.where(hit, 1.0, 0.0).astype(BF)
        return 0

    lax.fori_loop(0, vox // height, build, 0)

    edges = dot(gather_sel[...], stacked.astype(BF))
    position, slot = edges[:, :32], edges[:, 32:64]
    quad_of = lax.shift_right_logical(lax.broadcasted_iota(jnp.int32, position.shape, 0), 5)
    start = jnp.full(position.shape, FIRST[0], jnp.int32)
    for quad in range(1, 4):
        start = jnp.where(quad_of == quad, FIRST[quad], start)
    ahead = position - start.astype(F32)
    ahead = jnp.where(ahead < 0.0, ahead + len(RING), ahead)
    near = jnp.where(jnp.logical_and(position < 12.0, ahead < BESIDE), ahead * SLOT + slot, -1.0)
    for quad in range(4):
        halo_hot[quad, :SLOT, :] = jnp.zeros((SLOT, BESIDE * SLOT), BF)
        halo_hot[quad, (OFFS + 1) * SLOT :, :] = jnp.zeros((SLOT, BESIDE * SLOT), BF)
    row = lax.broadcasted_iota(jnp.int32, (4 * SLOT, BESIDE * SLOT), 1).astype(F32)
    for k in range(OFFS):
        hit = jnp.where(near[:, k : k + 1] == row, 1.0, 0.0).astype(BF)
        for quad in range(4):
            halo_hot[quad, (k + 1) * SLOT : (k + 2) * SLOT, :] = hit[
                quad * SLOT : (quad + 1) * SLOT
            ]

    def forward_weight(weight, forward):
        for k in range(OFFS):
            value = weight[k]
            forward[k * chan : (k + 1) * chan, :] = jnp.concatenate([value, value], axis=1)
        forward[width:, :] = jnp.zeros((chan, lanes), BF)

    def turned_weight(weight, turned):
        for j in range(PAIRS - 2):
            left = weight[2 * j]
            right = weight[2 * j + 1] if 2 * j + 1 < OFFS else jnp.zeros((chan, chan), BF)
            beside = jnp.concatenate([left, right], axis=1)
            turned[:chan, lanes * j : lanes * (j + 1)] = beside
            turned[chan:, lanes * j : lanes * (j + 1)] = beside

    def twice(bias):
        return jnp.concatenate([bias[...], bias[...]], axis=1)

    def ty_copy(g, d, c):
        to = lax.rem(ty + d, tys)
        at = pl.multiple_of(to * quarter + c * chunk, chunk)
        return pltpu.make_async_remote_copy(
            src_ref=part.at[g, pl.ds(at, chunk)],
            dst_ref=rs1.at[g, d, pl.ds(pl.multiple_of(c * chunk, chunk), chunk)],
            send_sem=s1.at[g, d, c],
            recv_sem=r1.at[g, d, c],
            device_id=device(tx, to),
            device_id_type=MESH,
        )

    def tile_copy(g, d):
        to = lax.rem(tx + d, tiles)
        at = pl.multiple_of(lax.rem(to, owners) * chunk, chunk)
        return pltpu.make_async_remote_copy(
            src_ref=mid.at[g, pl.ds(at, chunk)],
            dst_ref=rs2.at[g, d],
            send_sem=s2.at[g, d],
            recv_sem=r2.at[g, d],
            device_id=device(to, ty),
            device_id_type=MESH,
        )

    def chunk_rows(y, c):
        return pl.ds(pl.multiple_of(y * quarter + lax.rem(c, owners) * chunk, chunk), chunk)

    def back_tile(g, d, c):
        return pltpu.make_async_remote_copy(
            src_ref=full.at[g, chunk_rows(ty, c)],
            dst_ref=full.at[g, chunk_rows(ty, c)],
            send_sem=s3.at[g, d],
            recv_sem=r3.at[g, d],
            device_id=device(lax.rem(tx + d, tiles), ty),
            device_id_type=MESH,
        )

    def back_ty(g, d, y, c):
        at = lax.rem(c, owners)
        return pltpu.make_async_remote_copy(
            src_ref=full.at[g, chunk_rows(y, c)],
            dst_ref=full.at[g, chunk_rows(y, c)],
            send_sem=s4.at[g, d, at],
            recv_sem=r4.at[g, d, at],
            device_id=device(tx, lax.rem(ty + d, tys)),
            device_id_type=MESH,
        )

    def owned(x, body):
        if owners >= tiles:
            body()
        else:
            pl.when(x < owners)(body)

    def reduce_start(g, gradient, edge, own_picked, halo_picked):
        turned = gradient.astype(F32).T[:chan].astype(BF)
        edge_turned = edge.astype(F32).T[:chan].astype(BF)
        terms = dot(turned, own_picked[...]) + dot(edge_turned, halo_picked[...])
        for j in range(PAIRS - 2):
            part[g, j * chan : (j + 1) * chan, :] = terms[
                :, lanes * j : lanes * (j + 1)
            ].astype(BF)
        part[g, (PAIRS - 2) * chan :, :] = jnp.zeros((2 * chan, lanes), BF)
        for i in range(owners):
            for d in range(1, tys):
                ty_copy(g, d, lax.rem(tx + 1 + i, owners)).start()

    def reduce_tiles(g):
        for d in [*range(1, tiles), 0]:
            c = lax.rem(tx + d, tiles)

            def body():
                for e in range(1, tys):
                    ty_copy(g, e, lax.rem(c, owners)).wait_recv()
                total = part[g, chunk_rows(ty, c), :].astype(F32)
                rows = pl.ds(pl.multiple_of(lax.rem(c, owners) * chunk, chunk), chunk)
                for e in range(1, tys):
                    total = total + rs1[g, e, rows, :].astype(F32)
                turned = []
                for j in range(chunk // chan):
                    flat = total[j * chan : (j + 1) * chan].T
                    turned.append(jnp.concatenate([flat[:chan], flat[chan:]], axis=1))
                mid[g, rows, :] = jnp.concatenate(turned, axis=0).astype(BF)
                if d:
                    tile_copy(g, d).start()

            owned(c, body)

    def spread_tiles(g):
        def body():
            for d in range(1, tiles):
                tile_copy(g, d).wait_recv()
            at = pl.multiple_of(lax.rem(tx, owners) * chunk, chunk)
            total = mid[g, pl.ds(at, chunk), :].astype(F32)
            for d in range(1, tiles):
                total = total + rs2[g, d].astype(F32)
            full[g, chunk_rows(ty, tx), :] = total.astype(BF)
            for d in range(1, tiles):
                back_tile(g, d, tx).start()
            for d in range(1, tys):
                back_ty(g, d, ty, tx).start()

        owned(tx, body)

    def spread_ty(g):
        for d in range(1, tiles):
            source = lax.rem(tx - d + tiles, tiles)

            def body():
                back_tile(g, d, source).wait_recv()
                for e in range(1, tys):
                    back_ty(g, e, ty, source).start()

            owned(source, body)

    def finish(g):
        for d in range(1, tys):
            for c in range(owners):
                back_ty(g, d, lax.rem(ty - d + tys, tys), jnp.int32(c)).wait_recv()
        full_out[g] = full[g]

    def drain(g):
        for d in range(1, tys):
            for c in range(owners):
                ty_copy(g, d, c).wait_send()
                back_ty(g, d, ty, jnp.int32(c)).wait_send()
        for d in range(1, tiles):
            owned(lax.rem(tx + d, tiles), lambda: tile_copy(g, d).wait_send())
            owned(tx, lambda: back_tile(g, d, tx).wait_send())

    plain = ((1,), (0,))
    across = ((1,), (1,))
    pick_own(inputs.astype(BF), own_a, False)
    loads[3].wait()
    forward_weight(w1, wf1)
    wait_halo(0)
    pick_halo(0, halo_a, False)
    first = convolve(own_a, halo_a, wf1, plain) + twice(b1)
    hidden = (first * jax.nn.sigmoid(first)).astype(BF)
    send_halo(1, hidden)
    pick_own(hidden, own_b, False)
    loads[4].wait()
    loads[5].wait()
    forward_weight(w2, wf2)
    upstream = cot[...].astype(F32)
    upstream = jnp.concatenate([upstream, upstream], axis=0).T
    wait_halo(1)
    pick_halo(1, halo_b, False)
    second = convolve(own_b, halo_b, wf2, plain) + twice(b2)
    grad_out = (upstream * silu_slope(inputs + second)).astype(BF)

    send_halo(2, grad_out)
    reduce_start(1, grad_out, buckets[2], own_b, halo_b)
    pick_own(grad_out, own_c, True)
    turned_weight(w2, wt2)
    wait_halo(2)
    pick_halo(2, halo_c, True)
    back = convolve(own_c, halo_c, wt2, across)
    grad_pre = (back * silu_slope(first)).astype(BF)
    send_halo(3, grad_pre)
    reduce_start(0, grad_pre, buckets[3], own_a, halo_a)
    reduce_tiles(1)
    pick_own(grad_pre, own_c, True)
    turned_weight(w1, wt1)
    spread_tiles(1)
    wait_halo(3)
    pick_halo(3, halo_c, True)
    back = convolve(own_c, halo_c, wt1, across)
    gf_out[...] = (grad_out.astype(F32) + back).T[:chan]
    reduce_tiles(0)
    spread_ty(1)
    spread_tiles(0)
    spread_ty(0)
    finish(1)
    finish(0)
    for stage in range(4):
        wait_sent(stage)
    drain(1)
    drain(0)


def unpack(scale, gf, full, gf_out, gw1_out, gb1_out, gw2_out, gb2_out):
    gf_out[0, 0] = gf[...]
    chan = gf.shape[0]
    for g, gw_out, gb_out in ((0, gw1_out, gb1_out), (1, gw2_out, gb2_out)):
        for j in range(PAIRS - 2):
            value = full[g, j * chan : (j + 1) * chan, :].astype(F32) * scale
            gw_out[2 * j] = value[:, :chan]
            if 2 * j + 1 < OFFS:
                gw_out[2 * j + 1] = value[:, chan:]
            else:
                gb_out[...] = value[:1, chan:]


def per_device(feats, weight1, bias1, weight2, bias2, cotangent, neighbors, shell):
    tiles, chs, subs = (lax.axis_size(a) for a in ("tile", "ch", "sub"))
    chan, vox = feats.shape[2:]
    tys = chs * subs
    scale = 1.0 / math.sqrt(vox * tiles * tys)
    rows = PAIRS * chan
    quarter = rows // tys
    chunk = max(chan, quarter // tiles)
    owners = quarter // chunk
    wide = (PAIRS - 2) * 2 * chan
    lanes = 2 * chan
    edge = 4 * SLOT
    vmem = pl.BlockSpec(memory_space=pltpu.VMEM)
    hbm = pl.BlockSpec(memory_space=pl.ANY)
    dma = pltpu.SemaphoreType.DMA
    gf, full = pl.pallas_call(
        functools.partial(kernel, tiles, chs, subs),
        out_shape=(
            jax.ShapeDtypeStruct((chan, vox), F32),
            jax.ShapeDtypeStruct((2, rows, lanes), BF),
        ),
        in_specs=[hbm, hbm, vmem, hbm, vmem, hbm, hbm, hbm],
        out_specs=(vmem, vmem),
        scratch_shapes=[
            pltpu.VMEM((chan, vox), BF),
            pltpu.VMEM(weight1.shape, BF),
            pltpu.VMEM(weight2.shape, BF),
            pltpu.VMEM((chan, vox), BF),
            pltpu.VMEM((OFFS, vox), jnp.int32),
            pltpu.VMEM(shell.shape[2:], jnp.int32),
            dma((6,)),
            pltpu.VMEM(((OFFS + 2) * vox, vox), BF),
            pltpu.VMEM((4, (OFFS + 2) * SLOT, BESIDE * SLOT), BF),
            pltpu.VMEM((4, (len(RING) + 3) * SLOT, lanes), BF),
            pltpu.VMEM((vox, wide), BF),
            pltpu.VMEM((vox, wide), BF),
            pltpu.VMEM((vox, wide), BF),
            pltpu.VMEM((edge, wide), BF),
            pltpu.VMEM((edge, wide), BF),
            pltpu.VMEM((edge, wide), BF),
            pltpu.VMEM((wide, lanes), BF),
            pltpu.VMEM((wide, lanes), BF),
            pltpu.VMEM((lanes, wide), BF),
            pltpu.VMEM((lanes, wide), BF),
            pltpu.VMEM((edge, vox), BF),
            pltpu.VMEM((vox, 2 * edge), BF),
            pltpu.VMEM((4, edge, lanes), BF),
            pltpu.VMEM((vox, 128), F32),
            pltpu.VMEM((2, rows, lanes), BF),
            pltpu.VMEM((2, tys, quarter, lanes), BF),
            pltpu.VMEM((2, quarter, lanes), BF),
            pltpu.VMEM((2, tiles, chunk, lanes), BF),
            pltpu.VMEM((2, rows, lanes), BF),
            dma((4, len(RING))),
            dma((4, len(RING))),
            dma((2, tys, owners)),
            dma((2, tys, owners)),
            dma((2, tiles)),
            dma((2, tiles)),
            dma((2, tiles)),
            dma((2, tiles)),
            dma((2, tys, owners)),
            dma((2, tys, owners)),
        ],
        compiler_params=pltpu.CompilerParams(
            collective_id=0, has_side_effects=True, vmem_limit_bytes=48 * 1024 * 1024
        ),
    )(feats, weight1, bias1[None], weight2, bias2[None], cotangent, neighbors, shell)
    gf, gw1, gb1, gw2, gb2 = pl.pallas_call(
        functools.partial(unpack, scale),
        out_shape=(
            jax.ShapeDtypeStruct((1, 1, chan, vox), F32),
            jax.ShapeDtypeStruct((OFFS, chan, chan), F32),
            jax.ShapeDtypeStruct((1, chan), F32),
            jax.ShapeDtypeStruct((OFFS, chan, chan), F32),
            jax.ShapeDtypeStruct((1, chan), F32),
        ),
        in_specs=[vmem] * 2,
        out_specs=(vmem,) * 5,
        compiler_params=pltpu.CompilerParams(vmem_limit_bytes=16 * 1024 * 1024),
    )(gf, full)
    return gf, gw1, gb1[0], gw2, gb2[0]


def solution(mesh):
    placed = (
        P(("parts", "tile"), ("ch", "sub"), None, None),
        P(),
        P(),
        P(),
        P(),
        P(("parts", "tile"), ("ch", "sub"), None, None),
        P(("parts", "tile"), ("ch", "sub"), None, None),
        P(("parts", "tile"), ("ch", "sub"), None, None, None),
    )
    return jax.shard_map(
        per_device,
        mesh=mesh,
        in_specs=placed,
        out_specs=(
            P(("parts", "tile"), ("ch", "sub"), None, None),
            P("parts", None, None),
            P("parts"),
            P("parts", None, None),
            P("parts"),
        ),
        check_vma=False,
    )
```

```python
import functools
import math

import jax
import jax.numpy as jnp
from jax import lax
from jax.experimental import pallas as pl
from jax.experimental.pallas import tpu as pltpu
from jax.sharding import PartitionSpec as P

BF = jnp.bfloat16
F32 = jnp.float32
MESH = pl.DeviceIdType.MESH
SLOT = 32
PAIRS = 16
OFFS = 27
UNROLL = 14
RING = [
    (0, 0), (0, 1), (0, 2), (0, 3), (1, 3), (2, 3),
    (3, 3), (3, 2), (3, 1), (3, 0), (2, 0), (1, 0),
]
BESIDE = 5
FIRST = (10, 1, 7, 4)
SHIFT = (-1, 0, 0, 1)
HALF = (1, 0, 1, 0)


def dot(a, b, dims=((1,), (0,))):
    return lax.dot_general(a, b, (dims, ((), ())), preferred_element_type=F32)


def silu_slope(values):
    sigmoid = jax.nn.sigmoid(values)
    return sigmoid * (1.0 + values * (1.0 - sigmoid))


def kernel(
    tiles, chs, subs,
    feats_in, w1_in, b1_in, w2_in, b2_in, cot_in, nbr_in, shell_in,
    gf_out, full_out,
    feats, w1, b1, w2, b2, cot, nbr, shell, in_sem,
    own_hot, halo_hot, ring, own_a, own_b, own_c, halo_a, halo_b, halo_c,
    wf1, wf2, wt1, wt2, gather_sel, scatter_sel, buckets, table,
    part, rs1, mid, rs2, full,
    halo_send, halo_recv, s1, r1, s2, r2, s3, r3, s4, r4,
):
    vox = feats.shape[1]
    chan = feats.shape[0]
    lanes = 2 * chan
    width = OFFS * chan
    tys = chs * subs
    tx = lax.axis_index("tile")
    ty = lax.axis_index("ch") * subs + lax.axis_index("sub")
    quarter = PAIRS * chan // tys
    chunk = max(chan, quarter // tiles)
    owners = quarter // chunk

    loads = [
        pltpu.make_async_copy(src, dst, in_sem.at[i])
        for i, (src, dst) in enumerate((
            (feats_in.at[0, 0], feats),
            (shell_in.at[0, 0], shell),
            (nbr_in.at[:, 0], nbr),
            (w1_in, w1),
            (cot_in.at[0, 0], cot),
            (w2_in, w2),
            (b1_in, b1),
            (b2_in, b2),
        ))
    ]
    for load in loads:
        load.start()

    def device(x, y):
        return {"tile": x, "ch": y // subs, "sub": y % subs}

    def exists(dx, dy):
        ok = None
        for at, d, n in ((tx, dx, tiles), (ty, dy, tys)):
            if d:
                here = at > 0 if d < 0 else at < n - 1
                ok = here if ok is None else jnp.logical_and(ok, here)
        return ok

    for stage in range(4):
        ring[stage] = jnp.zeros(ring.shape[1:], BF)

    barrier = pltpu.get_barrier_semaphore()
    for dx in (-1, 0, 1):
        for dy in (-1, 0, 1):
            if dx or dy:

                @pl.when(exists(dx, dy))
                def _():
                    pl.semaphore_signal(
                        barrier, inc=1, device_id=device(tx + dx, ty + dy), device_id_type=MESH
                    )

    for d in range(1, tys):
        pl.semaphore_signal(
            barrier, inc=1, device_id=device(tx, lax.rem(ty + d, tys)), device_id_type=MESH
        )
    for d in range(1, tiles):
        pl.semaphore_signal(
            barrier, inc=1, device_id=device(lax.rem(tx + d, tiles), ty), device_id_type=MESH
        )
    near_x = 1 + jnp.minimum(tx, 1) + jnp.minimum(tiles - 1 - tx, 1)
    near_y = 1 + jnp.minimum(ty, 1) + jnp.minimum(tys - 1 - ty, 1)

    def halo_copy(stage, n):
        p, q = RING[n]
        quad = 2 * HALF[p] + HALF[q]
        return pltpu.make_async_remote_copy(
            src_ref=buckets.at[stage, pl.ds(quad * SLOT, SLOT)],
            dst_ref=ring.at[stage, pl.ds(n * SLOT, SLOT)],
            send_sem=halo_send.at[stage, n],
            recv_sem=halo_recv.at[stage, n],
            device_id=device(tx - SHIFT[p], ty - SHIFT[q]),
            device_id_type=MESH,
        )

    def outgoing(n):
        return exists(-SHIFT[RING[n][0]], -SHIFT[RING[n][1]])

    def incoming(n):
        return exists(SHIFT[RING[n][0]], SHIFT[RING[n][1]])

    def send_halo(stage, own):
        buckets[stage] = dot(gather_sel[...], own).astype(BF)
        for n in range(len(RING)):

            @pl.when(outgoing(n))
            def _():
                halo_copy(stage, n).start()

    def wait_halo(stage):
        for n in range(len(RING)):

            @pl.when(incoming(n))
            def _():
                halo_copy(stage, n).wait_recv()

        again = ring.shape[1] - len(RING) * SLOT
        ring[stage, len(RING) * SLOT :, :] = ring[stage, :again, :]

    def wait_sent(stage):
        for n in range(len(RING)):

            @pl.when(outgoing(n))
            def _():
                halo_copy(stage, n).wait_send()

    def pick_own(own, into, flip):
        low = lax.broadcasted_iota(jnp.int32, (vox, lanes), 1) < chan
        step = UNROLL

        def some(i, _):
            for u in range(step):
                j = i * step + u
                first = (OFFS - 1) - 2 * j if flip else 2 * j + 1
                rows = pl.ds(pl.multiple_of(first * vox, vox), 2 * vox)
                both = dot(own_hot[rows, :], own)
                ahead, behind = both[:vox], both[vox:]
                if flip:
                    ahead, behind = behind, ahead
                at = pl.multiple_of(j * lanes, lanes)
                into[:, pl.ds(at, lanes)] = jnp.where(low, ahead, behind).astype(BF)
            return 0

        lax.fori_loop(0, (PAIRS - 2) // step, some, 0)
        last = into[:, width - chan :]
        into[:, width - chan :] = jnp.where(low, last, jnp.ones_like(last))

    def pick_halo(stage, into, flip):
        low = lax.broadcasted_iota(jnp.int32, (SLOT, lanes), 1) < chan
        for quad in range(4):
            near = ring[stage, FIRST[quad] * SLOT : (FIRST[quad] + BESIDE) * SLOT, :]
            found = dot(halo_hot[quad], near)
            for j in range(PAIRS - 2):
                k0, k1 = (OFFS - 2 * j, OFFS - 1 - 2 * j) if flip else (2 * j + 1, 2 * j + 2)
                into[quad * SLOT : (quad + 1) * SLOT, j * lanes : (j + 1) * lanes] = jnp.where(
                    low, found[k0 * SLOT : (k0 + 1) * SLOT], found[k1 * SLOT : (k1 + 1) * SLOT]
                ).astype(BF)

    def convolve(own_picked, halo_picked, weight, dims):
        edge = dot(halo_picked[...], weight[...], dims)
        high = edge.astype(BF)
        low = (edge - high.astype(F32)).astype(BF)
        inner = dot(own_picked[...], weight[...], dims)
        return inner + dot(scatter_sel[...], jnp.concatenate([high, low], axis=0))

    loads[0].wait()
    loads[1].wait()
    quads = [shell[a, b : b + 1, :][:, :SLOT] for a in range(2) for b in range(2)]
    listed = jnp.concatenate(quads, axis=1)
    by_voxel = lax.broadcasted_iota(jnp.int32, (vox, 4 * SLOT), 0) == listed
    scatter = jnp.where(by_voxel, 1.0, 0.0)
    gather = scatter.T
    gather_sel[...] = gather.astype(BF)
    scatter_sel[...] = jnp.concatenate([scatter, scatter], axis=1).astype(BF)

    both = feats[...].astype(F32)
    inputs = jnp.concatenate([both, both], axis=0).T
    pl.semaphore_wait(barrier, near_x * near_y - 1 + (tys - 1) + (tiles - 1))
    send_halo(0, inputs.astype(BF))

    loads[2].wait()
    index = nbr[...]
    outer = index - vox
    slot = jnp.bitwise_and(outer, 127)
    block = lax.shift_right_logical(outer, 7)
    position = jnp.full(index.shape, 15, jnp.int32)
    for n, (p, q) in enumerate(RING):
        position = jnp.where(block == 4 * p + q, n, position)
    position = jnp.where(jnp.logical_and(index >= vox, slot < SLOT), position, 15)
    slot = jnp.bitwise_and(slot, SLOT - 1)
    fill = jnp.zeros((32 - OFFS, vox), F32)
    stacked = [position.astype(F32), fill, slot.astype(F32), fill, index.astype(F32), fill]
    stacked = jnp.concatenate(stacked + [jnp.zeros((32, vox), F32)], axis=0).T
    table[...] = stacked

    place = lax.broadcasted_iota(jnp.int32, (4 * SLOT, vox), 0)
    quad_of = lax.shift_right_logical(place, 5)
    frame_block = 5 + 4 * lax.shift_right_logical(quad_of, 1) + jnp.bitwise_and(quad_of, 1)
    frame_row = vox + 128 * frame_block + jnp.bitwise_and(place, SLOT - 1)
    alias = jnp.where(gather > 0.5, frame_row.astype(F32), -1.0)
    alias = jnp.max(alias, axis=0, keepdims=True)
    own_hot[:vox, :] = jnp.zeros((vox, vox), BF)
    own_hot[(OFFS + 1) * vox :, :] = jnp.zeros((vox, vox), BF)
    height = 32

    def build(i, _):
        base = i * height
        entries = table[pl.ds(pl.multiple_of(base, height), height), :]
        row = lax.broadcasted_iota(jnp.int32, (height, vox), 1).astype(F32)
        for k in range(OFFS):
            entry = entries[:, 64 + k : 65 + k]
            hit = jnp.logical_or(entry == row, entry == alias)
            at = pl.multiple_of((k + 1) * vox + base, height)
            own_hot[pl.ds(at, height), :] = jnp.where(hit, 1.0, 0.0).astype(BF)
        return 0

    lax.fori_loop(0, vox // height, build, 0)

    edges = dot(gather_sel[...], stacked.astype(BF))
    position, slot = edges[:, :32], edges[:, 32:64]
    quad_of = lax.shift_right_logical(lax.broadcasted_iota(jnp.int32, position.shape, 0), 5)
    start = jnp.full(position.shape, FIRST[0], jnp.int32)
    for quad in range(1, 4):
        start = jnp.where(quad_of == quad, FIRST[quad], start)
    ahead = position - start.astype(F32)
    ahead = jnp.where(ahead < 0.0, ahead + len(RING), ahead)
    near = jnp.where(jnp.logical_and(position < 12.0, ahead < BESIDE), ahead * SLOT + slot, -1.0)
    for quad in range(4):
        halo_hot[quad, :SLOT, :] = jnp.zeros((SLOT, BESIDE * SLOT), BF)
        halo_hot[quad, (OFFS + 1) * SLOT :, :] = jnp.zeros((SLOT, BESIDE * SLOT), BF)
    row = lax.broadcasted_iota(jnp.int32, (4 * SLOT, BESIDE * SLOT), 1).astype(F32)
    for k in range(OFFS):
        hit = jnp.where(near[:, k : k + 1] == row, 1.0, 0.0).astype(BF)
        for quad in range(4):
            halo_hot[quad, (k + 1) * SLOT : (k + 2) * SLOT, :] = hit[
                quad * SLOT : (quad + 1) * SLOT
            ]

    def forward_weight(weight, forward):
        for k in range(OFFS):
            value = weight[k]
            forward[k * chan : (k + 1) * chan, :] = jnp.concatenate([value, value], axis=1)
        forward[width:, :] = jnp.zeros((chan, lanes), BF)

    def turned_weight(weight, turned):
        for j in range(PAIRS - 2):
            left = weight[2 * j]
            right = weight[2 * j + 1] if 2 * j + 1 < OFFS else jnp.zeros((chan, chan), BF)
            beside = jnp.concatenate([left, right], axis=1)
            turned[:chan, lanes * j : lanes * (j + 1)] = beside
            turned[chan:, lanes * j : lanes * (j + 1)] = beside

    def twice(bias):
        return jnp.concatenate([bias[...], bias[...]], axis=1)

    def ty_copy(g, d, c):
        to = lax.rem(ty + d, tys)
        at = pl.multiple_of(to * quarter + c * chunk, chunk)
        return pltpu.make_async_remote_copy(
            src_ref=part.at[g, pl.ds(at, chunk)],
            dst_ref=rs1.at[g, d, pl.ds(pl.multiple_of(c * chunk, chunk), chunk)],
            send_sem=s1.at[g, d, c],
            recv_sem=r1.at[g, d, c],
            device_id=device(tx, to),
            device_id_type=MESH,
        )

    def tile_copy(g, d):
        to = lax.rem(tx + d, tiles)
        at = pl.multiple_of(lax.rem(to, owners) * chunk, chunk)
        return pltpu.make_async_remote_copy(
            src_ref=mid.at[g, pl.ds(at, chunk)],
            dst_ref=rs2.at[g, d],
            send_sem=s2.at[g, d],
            recv_sem=r2.at[g, d],
            device_id=device(to, ty),
            device_id_type=MESH,
        )

    def chunk_rows(y, c):
        return pl.ds(pl.multiple_of(y * quarter + lax.rem(c, owners) * chunk, chunk), chunk)

    def back_tile(g, d, c):
        return pltpu.make_async_remote_copy(
            src_ref=full.at[g, chunk_rows(ty, c)],
            dst_ref=full.at[g, chunk_rows(ty, c)],
            send_sem=s3.at[g, d],
            recv_sem=r3.at[g, d],
            device_id=device(lax.rem(tx + d, tiles), ty),
            device_id_type=MESH,
        )

    def back_ty(g, d, y, c):
        at = lax.rem(c, owners)
        return pltpu.make_async_remote_copy(
            src_ref=full.at[g, chunk_rows(y, c)],
            dst_ref=full.at[g, chunk_rows(y, c)],
            send_sem=s4.at[g, d, at],
            recv_sem=r4.at[g, d, at],
            device_id=device(tx, lax.rem(ty + d, tys)),
            device_id_type=MESH,
        )

    def owned(x, body):
        if owners >= tiles:
            body()
        else:
            pl.when(x < owners)(body)

    def reduce_start(g, gradient, edge, own_picked, halo_picked):
        turned = gradient.astype(F32).T[:chan].astype(BF)
        edge_turned = edge.astype(F32).T[:chan].astype(BF)
        terms = dot(turned, own_picked[...]) + dot(edge_turned, halo_picked[...])
        for j in range(PAIRS - 2):
            part[g, j * chan : (j + 1) * chan, :] = terms[
                :, lanes * j : lanes * (j + 1)
            ].astype(BF)
        part[g, (PAIRS - 2) * chan :, :] = jnp.zeros((2 * chan, lanes), BF)
        for i in range(owners):
            for d in range(1, tys):
                ty_copy(g, d, lax.rem(tx + 1 + i, owners)).start()

    def reduce_tiles(g):
        for d in [*range(1, tiles), 0]:
            c = lax.rem(tx + d, tiles)

            def body():
                for e in range(1, tys):
                    ty_copy(g, e, lax.rem(c, owners)).wait_recv()
                total = part[g, chunk_rows(ty, c), :].astype(F32)
                rows = pl.ds(pl.multiple_of(lax.rem(c, owners) * chunk, chunk), chunk)
                for e in range(1, tys):
                    total = total + rs1[g, e, rows, :].astype(F32)
                turned = []
                for j in range(chunk // chan):
                    flat = total[j * chan : (j + 1) * chan].T
                    turned.append(jnp.concatenate([flat[:chan], flat[chan:]], axis=1))
                mid[g, rows, :] = jnp.concatenate(turned, axis=0).astype(BF)
                if d:
                    tile_copy(g, d).start()

            owned(c, body)

    def spread_tiles(g):
        def body():
            for d in range(1, tiles):
                tile_copy(g, d).wait_recv()
            at = pl.multiple_of(lax.rem(tx, owners) * chunk, chunk)
            total = mid[g, pl.ds(at, chunk), :].astype(F32)
            for d in range(1, tiles):
                total = total + rs2[g, d].astype(F32)
            full[g, chunk_rows(ty, tx), :] = total.astype(BF)
            for d in range(1, tiles):
                back_tile(g, d, tx).start()
            for d in range(1, tys):
                back_ty(g, d, ty, tx).start()

        owned(tx, body)

    def spread_ty(g):
        for d in range(1, tiles):
            source = lax.rem(tx - d + tiles, tiles)

            def body():
                back_tile(g, d, source).wait_recv()
                for e in range(1, tys):
                    back_ty(g, e, ty, source).start()

            owned(source, body)

    def finish(g):
        for d in range(1, tys):
            for c in range(owners):
                back_ty(g, d, lax.rem(ty - d + tys, tys), jnp.int32(c)).wait_recv()
        full_out[g] = full[g]

    def drain_sums(g):
        for d in range(1, tys):
            for c in range(owners):
                ty_copy(g, d, c).wait_send()
        for d in range(1, tiles):
            owned(lax.rem(tx + d, tiles), lambda: tile_copy(g, d).wait_send())

    def drain_back(g):
        for d in range(1, tys):
            for c in range(owners):
                back_ty(g, d, ty, jnp.int32(c)).wait_send()
        for d in range(1, tiles):
            owned(tx, lambda: back_tile(g, d, tx).wait_send())

    plain = ((1,), (0,))
    across = ((1,), (1,))
    pick_own(inputs.astype(BF), own_a, False)
    loads[3].wait()
    forward_weight(w1, wf1)
    loads[6].wait()
    loads[7].wait()
    wait_halo(0)
    pick_halo(0, halo_a, False)
    first = convolve(own_a, halo_a, wf1, plain) + twice(b1)
    hidden = (first * jax.nn.sigmoid(first)).astype(BF)
    send_halo(1, hidden)
    pick_own(hidden, own_b, False)
    loads[4].wait()
    loads[5].wait()
    forward_weight(w2, wf2)
    turned_weight(w2, wt2)
    upstream = cot[...].astype(F32)
    upstream = jnp.concatenate([upstream, upstream], axis=0).T
    wait_halo(1)
    pick_halo(1, halo_b, False)
    second = convolve(own_b, halo_b, wf2, plain) + twice(b2)
    grad_out = (upstream * silu_slope(inputs + second)).astype(BF)

    send_halo(2, grad_out)
    reduce_start(1, grad_out, buckets[2], own_b, halo_b)
    pick_own(grad_out, own_c, True)
    turned_weight(w1, wt1)
    wait_halo(2)
    pick_halo(2, halo_c, True)
    back = convolve(own_c, halo_c, wt2, across)
    grad_pre = (back * silu_slope(first)).astype(BF)
    send_halo(3, grad_pre)
    reduce_start(0, grad_pre, buckets[3], own_a, halo_a)
    reduce_tiles(1)
    pick_own(grad_pre, own_c, True)
    spread_tiles(1)
    wait_halo(3)
    pick_halo(3, halo_c, True)
    reduce_tiles(0)
    spread_ty(1)
    back = convolve(own_c, halo_c, wt1, across)
    gf_out[...] = (grad_out.astype(F32) + back).T[:chan]
    spread_tiles(0)
    for stage in range(4):
        wait_sent(stage)
    drain_sums(1)
    spread_ty(0)
    drain_sums(0)
    finish(1)
    drain_back(1)
    finish(0)
    drain_back(0)


def unpack(scale, gf, full, gf_out, gw1_out, gb1_out, gw2_out, gb2_out):
    gf_out[0, 0] = gf[...]
    chan = gf.shape[0]
    for g, gw_out, gb_out in ((0, gw1_out, gb1_out), (1, gw2_out, gb2_out)):
        for j in range(PAIRS - 2):
            value = full[g, j * chan : (j + 1) * chan, :].astype(F32) * scale
            gw_out[2 * j] = value[:, :chan]
            if 2 * j + 1 < OFFS:
                gw_out[2 * j + 1] = value[:, chan:]
            else:
                gb_out[...] = value[:1, chan:]


def per_device(feats, weight1, bias1, weight2, bias2, cotangent, neighbors, shell):
    tiles, chs, subs = (lax.axis_size(a) for a in ("tile", "ch", "sub"))
    chan, vox = feats.shape[2:]
    tys = chs * subs
    scale = 1.0 / math.sqrt(vox * tiles * tys)
    rows = PAIRS * chan
    quarter = rows // tys
    chunk = max(chan, quarter // tiles)
    owners = quarter // chunk
    wide = (PAIRS - 2) * 2 * chan
    lanes = 2 * chan
    edge = 4 * SLOT
    vmem = pl.BlockSpec(memory_space=pltpu.VMEM)
    hbm = pl.BlockSpec(memory_space=pltpu.HBM)
    dma = pltpu.SemaphoreType.DMA
    gf, full = pl.pallas_call(
        functools.partial(kernel, tiles, chs, subs),
        out_shape=(
            jax.ShapeDtypeStruct((chan, vox), F32),
            jax.ShapeDtypeStruct((2, rows, lanes), BF),
        ),
        in_specs=[hbm] * 8,
        out_specs=(vmem, vmem),
        scratch_shapes=[
            pltpu.VMEM((chan, vox), BF),
            pltpu.VMEM(weight1.shape, BF),
            pltpu.VMEM((1, chan), F32),
            pltpu.VMEM(weight2.shape, BF),
            pltpu.VMEM((1, chan), F32),
            pltpu.VMEM((chan, vox), BF),
            pltpu.VMEM((OFFS, vox), jnp.int32),
            pltpu.VMEM(shell.shape[2:], jnp.int32),
            dma((8,)),
            pltpu.VMEM(((OFFS + 2) * vox, vox), BF),
            pltpu.VMEM((4, (OFFS + 2) * SLOT, BESIDE * SLOT), BF),
            pltpu.VMEM((4, (len(RING) + 3) * SLOT, lanes), BF),
            pltpu.VMEM((vox, wide), BF),
            pltpu.VMEM((vox, wide), BF),
            pltpu.VMEM((vox, wide), BF),
            pltpu.VMEM((edge, wide), BF),
            pltpu.VMEM((edge, wide), BF),
            pltpu.VMEM((edge, wide), BF),
            pltpu.VMEM((wide, lanes), BF),
            pltpu.VMEM((wide, lanes), BF),
            pltpu.VMEM((lanes, wide), BF),
            pltpu.VMEM((lanes, wide), BF),
            pltpu.VMEM((edge, vox), BF),
            pltpu.VMEM((vox, 2 * edge), BF),
            pltpu.VMEM((4, edge, lanes), BF),
            pltpu.VMEM((vox, 128), F32),
            pltpu.VMEM((2, rows, lanes), BF),
            pltpu.VMEM((2, tys, quarter, lanes), BF),
            pltpu.VMEM((2, quarter, lanes), BF),
            pltpu.VMEM((2, tiles, chunk, lanes), BF),
            pltpu.VMEM((2, rows, lanes), BF),
            dma((4, len(RING))),
            dma((4, len(RING))),
            dma((2, tys, owners)),
            dma((2, tys, owners)),
            dma((2, tiles)),
            dma((2, tiles)),
            dma((2, tiles)),
            dma((2, tiles)),
            dma((2, tys, owners)),
            dma((2, tys, owners)),
        ],
        compiler_params=pltpu.CompilerParams(
            collective_id=0, has_side_effects=True, vmem_limit_bytes=63 * 1024 * 1024
        ),
    )(feats, weight1, bias1[None], weight2, bias2[None], cotangent, neighbors.reshape(OFFS, 1, vox), shell)
    gf, gw1, gb1, gw2, gb2 = pl.pallas_call(
        functools.partial(unpack, scale),
        out_shape=(
            jax.ShapeDtypeStruct((1, 1, chan, vox), F32),
            jax.ShapeDtypeStruct((OFFS, chan, chan), F32),
            jax.ShapeDtypeStruct((1, chan), F32),
            jax.ShapeDtypeStruct((OFFS, chan, chan), F32),
            jax.ShapeDtypeStruct((1, chan), F32),
        ),
        in_specs=[vmem] * 2,
        out_specs=(vmem,) * 5,
        compiler_params=pltpu.CompilerParams(vmem_limit_bytes=16 * 1024 * 1024),
    )(gf, full)
    return gf, gw1, gb1[0], gw2, gb2[0]


def solution(mesh):
    placed = (
        P(("parts", "tile"), ("ch", "sub"), None, None),
        P(),
        P(),
        P(),
        P(),
        P(("parts", "tile"), ("ch", "sub"), None, None),
        P(("parts", "tile"), ("ch", "sub"), None, None),
        P(("parts", "tile"), ("ch", "sub"), None, None, None),
    )
    return jax.shard_map(
        per_device,
        mesh=mesh,
        in_specs=placed,
        out_specs=(
            P(("parts", "tile"), ("ch", "sub"), None, None),
            P("parts", None, None),
            P("parts"),
            P("parts", None, None),
            P("parts"),
        ),
        check_vma=False,
    )
```

```python
import functools
import math

import jax
import jax.numpy as jnp
from jax import lax
from jax.experimental import pallas as pl
from jax.experimental.pallas import tpu as pltpu
from jax.sharding import PartitionSpec as P

BF = jnp.bfloat16
F32 = jnp.float32
MESH = pl.DeviceIdType.MESH
SLOT = 32
PAIRS = 16
OFFS = 27
UNROLL = 14
RING = [
    (0, 0), (0, 1), (0, 2), (0, 3), (1, 3), (2, 3),
    (3, 3), (3, 2), (3, 1), (3, 0), (2, 0), (1, 0),
]
BESIDE = 5
FIRST = (10, 1, 7, 4)
SHIFT = (-1, 0, 0, 1)
HALF = (1, 0, 1, 0)


def dot(a, b, dims=((1,), (0,))):
    return lax.dot_general(a, b, (dims, ((), ())), preferred_element_type=F32)


def silu_slope(values):
    sigmoid = jax.nn.sigmoid(values)
    return sigmoid * (1.0 + values * (1.0 - sigmoid))


def kernel(
    tiles, chs, subs,
    feats_in, w1_in, b1_in, w2_in, b2_in, cot_in, nbr_in, shell_in,
    gf_out, full_out,
    feats, w1, b1, w2, b2, cot, nbr, shell, in_sem, gf, out_sem,
    own_hot, halo_hot, ring, own_a, own_b, own_c, halo_a, halo_b, halo_c,
    wf1, wf2, wt1, wt2, gather_sel, scatter_sel, buckets, table,
    part, rs1, mid, rs2, full,
    halo_send, halo_recv, s1, r1, s2, r2, s3, r3, s4, r4,
):
    vox = feats.shape[1]
    chan = feats.shape[0]
    lanes = 2 * chan
    width = OFFS * chan
    tys = chs * subs
    tx = lax.axis_index("tile")
    ty = lax.axis_index("ch") * subs + lax.axis_index("sub")
    quarter = PAIRS * chan // tys
    chunk = max(chan, quarter // tiles)
    owners = quarter // chunk

    loads = [
        pltpu.make_async_copy(src, dst, in_sem.at[i])
        for i, (src, dst) in enumerate((
            (feats_in.at[0, 0], feats),
            (shell_in.at[0, 0], shell),
            (nbr_in.at[:, 0], nbr),
            (w1_in, w1),
            (cot_in.at[0, 0], cot),
            (w2_in, w2),
            (b1_in, b1),
            (b2_in, b2),
        ))
    ]
    for load in loads:
        load.start()
    stores = [
        pltpu.make_async_copy(src, dst, out_sem.at[i])
        for i, (src, dst) in enumerate((
            (full.at[0], full_out.at[0]),
            (full.at[1], full_out.at[1]),
            (gf, gf_out),
        ))
    ]

    def device(x, y):
        return {"tile": x, "ch": y // subs, "sub": y % subs}

    def exists(dx, dy):
        ok = None
        for at, d, n in ((tx, dx, tiles), (ty, dy, tys)):
            if d:
                here = at > 0 if d < 0 else at < n - 1
                ok = here if ok is None else jnp.logical_and(ok, here)
        return ok

    for stage in range(4):
        ring[stage] = jnp.zeros(ring.shape[1:], BF)

    barrier = pltpu.get_barrier_semaphore()
    for dx in (-1, 0, 1):
        for dy in (-1, 0, 1):
            if dx or dy:

                @pl.when(exists(dx, dy))
                def _():
                    pl.semaphore_signal(
                        barrier, inc=1, device_id=device(tx + dx, ty + dy), device_id_type=MESH
                    )

    for d in range(1, tys):
        pl.semaphore_signal(
            barrier, inc=1, device_id=device(tx, lax.rem(ty + d, tys)), device_id_type=MESH
        )
    for d in range(1, tiles):
        pl.semaphore_signal(
            barrier, inc=1, device_id=device(lax.rem(tx + d, tiles), ty), device_id_type=MESH
        )
    near_x = 1 + jnp.minimum(tx, 1) + jnp.minimum(tiles - 1 - tx, 1)
    near_y = 1 + jnp.minimum(ty, 1) + jnp.minimum(tys - 1 - ty, 1)

    def halo_copy(stage, n):
        p, q = RING[n]
        quad = 2 * HALF[p] + HALF[q]
        return pltpu.make_async_remote_copy(
            src_ref=buckets.at[stage, pl.ds(quad * SLOT, SLOT)],
            dst_ref=ring.at[stage, pl.ds(n * SLOT, SLOT)],
            send_sem=halo_send.at[stage, n],
            recv_sem=halo_recv.at[stage, n],
            device_id=device(tx - SHIFT[p], ty - SHIFT[q]),
            device_id_type=MESH,
        )

    def outgoing(n):
        return exists(-SHIFT[RING[n][0]], -SHIFT[RING[n][1]])

    def incoming(n):
        return exists(SHIFT[RING[n][0]], SHIFT[RING[n][1]])

    def send_halo(stage, own):
        buckets[stage] = dot(gather_sel[...], own).astype(BF)
        for n in range(len(RING)):

            @pl.when(outgoing(n))
            def _():
                halo_copy(stage, n).start()

    def wait_halo(stage):
        for n in range(len(RING)):

            @pl.when(incoming(n))
            def _():
                halo_copy(stage, n).wait_recv()

        again = ring.shape[1] - len(RING) * SLOT
        ring[stage, len(RING) * SLOT :, :] = ring[stage, :again, :]

    def wait_sent(stage):
        for n in range(len(RING)):

            @pl.when(outgoing(n))
            def _():
                halo_copy(stage, n).wait_send()

    def pick_own(own, into, flip):
        low = lax.broadcasted_iota(jnp.int32, (vox, lanes), 1) < chan
        step = UNROLL

        def some(i, _):
            for u in range(step):
                j = i * step + u
                first = (OFFS - 1) - 2 * j if flip else 2 * j + 1
                rows = pl.ds(pl.multiple_of(first * vox, vox), 2 * vox)
                both = dot(own_hot[rows, :], own)
                ahead, behind = both[:vox], both[vox:]
                if flip:
                    ahead, behind = behind, ahead
                at = pl.multiple_of(j * lanes, lanes)
                into[:, pl.ds(at, lanes)] = jnp.where(low, ahead, behind).astype(BF)
            return 0

        lax.fori_loop(0, (PAIRS - 2) // step, some, 0)
        last = into[:, width - chan :]
        into[:, width - chan :] = jnp.where(low, last, jnp.ones_like(last))

    def pick_halo(stage, into, flip):
        low = lax.broadcasted_iota(jnp.int32, (SLOT, lanes), 1) < chan
        for quad in range(4):
            near = ring[stage, FIRST[quad] * SLOT : (FIRST[quad] + BESIDE) * SLOT, :]
            found = dot(halo_hot[quad], near)
            for j in range(PAIRS - 2):
                k0, k1 = (OFFS - 2 * j, OFFS - 1 - 2 * j) if flip else (2 * j + 1, 2 * j + 2)
                into[quad * SLOT : (quad + 1) * SLOT, j * lanes : (j + 1) * lanes] = jnp.where(
                    low, found[k0 * SLOT : (k0 + 1) * SLOT], found[k1 * SLOT : (k1 + 1) * SLOT]
                ).astype(BF)

    def convolve(own_picked, halo_picked, weight, dims):
        edge = dot(halo_picked[...], weight[...], dims)
        high = edge.astype(BF)
        low = (edge - high.astype(F32)).astype(BF)
        inner = dot(own_picked[...], weight[...], dims)
        return inner + dot(scatter_sel[...], jnp.concatenate([high, low], axis=0))

    loads[0].wait()
    loads[1].wait()
    quads = [shell[a, b : b + 1, :][:, :SLOT] for a in range(2) for b in range(2)]
    listed = jnp.concatenate(quads, axis=1)
    by_voxel = lax.broadcasted_iota(jnp.int32, (vox, 4 * SLOT), 0) == listed
    scatter = jnp.where(by_voxel, 1.0, 0.0)
    gather = scatter.T
    gather_sel[...] = gather.astype(BF)
    scatter_sel[...] = jnp.concatenate([scatter, scatter], axis=1).astype(BF)

    both = feats[...].astype(F32)
    inputs = jnp.concatenate([both, both], axis=0).T
    pl.semaphore_wait(barrier, near_x * near_y - 1 + (tys - 1) + (tiles - 1))
    send_halo(0, inputs.astype(BF))

    loads[2].wait()
    index = nbr[...]
    outer = index - vox
    slot = jnp.bitwise_and(outer, 127)
    block = lax.shift_right_logical(outer, 7)
    position = jnp.full(index.shape, 15, jnp.int32)
    for n, (p, q) in enumerate(RING):
        position = jnp.where(block == 4 * p + q, n, position)
    position = jnp.where(jnp.logical_and(index >= vox, slot < SLOT), position, 15)
    slot = jnp.bitwise_and(slot, SLOT - 1)
    fill = jnp.zeros((32 - OFFS, vox), F32)
    stacked = [position.astype(F32), fill, slot.astype(F32), fill, index.astype(F32), fill]
    stacked = jnp.concatenate(stacked + [jnp.zeros((32, vox), F32)], axis=0).T
    table[...] = stacked

    place = lax.broadcasted_iota(jnp.int32, (4 * SLOT, vox), 0)
    quad_of = lax.shift_right_logical(place, 5)
    frame_block = 5 + 4 * lax.shift_right_logical(quad_of, 1) + jnp.bitwise_and(quad_of, 1)
    frame_row = vox + 128 * frame_block + jnp.bitwise_and(place, SLOT - 1)
    alias = jnp.where(gather > 0.5, frame_row.astype(F32), -1.0)
    alias = jnp.max(alias, axis=0, keepdims=True)
    own_hot[:vox, :] = jnp.zeros((vox, vox), BF)
    own_hot[(OFFS + 1) * vox :, :] = jnp.zeros((vox, vox), BF)
    height = 32

    def build(i, _):
        base = i * height
        entries = table[pl.ds(pl.multiple_of(base, height), height), :]
        row = lax.broadcasted_iota(jnp.int32, (height, vox), 1).astype(F32)
        for k in range(OFFS):
            entry = entries[:, 64 + k : 65 + k]
            hit = jnp.logical_or(entry == row, entry == alias)
            at = pl.multiple_of((k + 1) * vox + base, height)
            own_hot[pl.ds(at, height), :] = jnp.where(hit, 1.0, 0.0).astype(BF)
        return 0

    lax.fori_loop(0, vox // height, build, 0)

    edges = dot(gather_sel[...], stacked.astype(BF))
    position, slot = edges[:, :32], edges[:, 32:64]
    quad_of = lax.shift_right_logical(lax.broadcasted_iota(jnp.int32, position.shape, 0), 5)
    start = jnp.full(position.shape, FIRST[0], jnp.int32)
    for quad in range(1, 4):
        start = jnp.where(quad_of == quad, FIRST[quad], start)
    ahead = position - start.astype(F32)
    ahead = jnp.where(ahead < 0.0, ahead + len(RING), ahead)
    near = jnp.where(jnp.logical_and(position < 12.0, ahead < BESIDE), ahead * SLOT + slot, -1.0)
    for quad in range(4):
        halo_hot[quad, :SLOT, :] = jnp.zeros((SLOT, BESIDE * SLOT), BF)
        halo_hot[quad, (OFFS + 1) * SLOT :, :] = jnp.zeros((SLOT, BESIDE * SLOT), BF)
    row = lax.broadcasted_iota(jnp.int32, (4 * SLOT, BESIDE * SLOT), 1).astype(F32)
    for k in range(OFFS):
        hit = jnp.where(near[:, k : k + 1] == row, 1.0, 0.0).astype(BF)
        for quad in range(4):
            halo_hot[quad, (k + 1) * SLOT : (k + 2) * SLOT, :] = hit[
                quad * SLOT : (quad + 1) * SLOT
            ]

    def forward_weight(weight, forward):
        for k in range(OFFS):
            value = weight[k]
            forward[k * chan : (k + 1) * chan, :] = jnp.concatenate([value, value], axis=1)
        forward[width:, :] = jnp.zeros((chan, lanes), BF)

    def turned_weight(weight, turned):
        for j in range(PAIRS - 2):
            left = weight[2 * j]
            right = weight[2 * j + 1] if 2 * j + 1 < OFFS else jnp.zeros((chan, chan), BF)
            beside = jnp.concatenate([left, right], axis=1)
            turned[:chan, lanes * j : lanes * (j + 1)] = beside
            turned[chan:, lanes * j : lanes * (j + 1)] = beside

    def twice(bias):
        return jnp.concatenate([bias[...], bias[...]], axis=1)

    def ty_copy(g, d, c):
        to = lax.rem(ty + d, tys)
        at = pl.multiple_of(to * quarter + c * chunk, chunk)
        return pltpu.make_async_remote_copy(
            src_ref=part.at[g, pl.ds(at, chunk)],
            dst_ref=rs1.at[g, d, pl.ds(pl.multiple_of(c * chunk, chunk), chunk)],
            send_sem=s1.at[g, d, c],
            recv_sem=r1.at[g, d, c],
            device_id=device(tx, to),
            device_id_type=MESH,
        )

    def tile_copy(g, d):
        to = lax.rem(tx + d, tiles)
        at = pl.multiple_of(lax.rem(to, owners) * chunk, chunk)
        return pltpu.make_async_remote_copy(
            src_ref=mid.at[g, pl.ds(at, chunk)],
            dst_ref=rs2.at[g, d],
            send_sem=s2.at[g, d],
            recv_sem=r2.at[g, d],
            device_id=device(to, ty),
            device_id_type=MESH,
        )

    def chunk_rows(y, c):
        return pl.ds(pl.multiple_of(y * quarter + lax.rem(c, owners) * chunk, chunk), chunk)

    def back_tile(g, d, c):
        return pltpu.make_async_remote_copy(
            src_ref=full.at[g, chunk_rows(ty, c)],
            dst_ref=full.at[g, chunk_rows(ty, c)],
            send_sem=s3.at[g, d],
            recv_sem=r3.at[g, d],
            device_id=device(lax.rem(tx + d, tiles), ty),
            device_id_type=MESH,
        )

    def back_ty(g, d, y, c):
        at = lax.rem(c, owners)
        return pltpu.make_async_remote_copy(
            src_ref=full.at[g, chunk_rows(y, c)],
            dst_ref=full.at[g, chunk_rows(y, c)],
            send_sem=s4.at[g, d, at],
            recv_sem=r4.at[g, d, at],
            device_id=device(tx, lax.rem(ty + d, tys)),
            device_id_type=MESH,
        )

    def owned(x, body):
        if owners >= tiles:
            body()
        else:
            pl.when(x < owners)(body)

    def reduce_start(g, gradient, edge, own_picked, halo_picked):
        turned = gradient.astype(F32).T[:chan].astype(BF)
        edge_turned = edge.astype(F32).T[:chan].astype(BF)
        terms = dot(turned, own_picked[...]) + dot(edge_turned, halo_picked[...])
        for j in range(PAIRS - 2):
            part[g, j * chan : (j + 1) * chan, :] = terms[
                :, lanes * j : lanes * (j + 1)
            ].astype(BF)
        part[g, (PAIRS - 2) * chan :, :] = jnp.zeros((2 * chan, lanes), BF)
        for i in range(owners):
            for d in range(1, tys):
                ty_copy(g, d, lax.rem(tx + 1 + i, owners)).start()

    def reduce_tiles(g):
        for d in [*range(1, tiles), 0]:
            c = lax.rem(tx + d, tiles)

            def body():
                for e in range(1, tys):
                    ty_copy(g, e, lax.rem(c, owners)).wait_recv()
                total = part[g, chunk_rows(ty, c), :].astype(F32)
                rows = pl.ds(pl.multiple_of(lax.rem(c, owners) * chunk, chunk), chunk)
                for e in range(1, tys):
                    total = total + rs1[g, e, rows, :].astype(F32)
                turned = []
                for j in range(chunk // chan):
                    flat = total[j * chan : (j + 1) * chan].T
                    turned.append(jnp.concatenate([flat[:chan], flat[chan:]], axis=1))
                mid[g, rows, :] = jnp.concatenate(turned, axis=0).astype(BF)
                if d:
                    tile_copy(g, d).start()

            owned(c, body)

    def spread_tiles(g):
        def body():
            for d in range(1, tiles):
                tile_copy(g, d).wait_recv()
            at = pl.multiple_of(lax.rem(tx, owners) * chunk, chunk)
            total = mid[g, pl.ds(at, chunk), :].astype(F32)
            for d in range(1, tiles):
                total = total + rs2[g, d].astype(F32)
            full[g, chunk_rows(ty, tx), :] = total.astype(BF)
            for d in range(1, tiles):
                back_tile(g, d, tx).start()
            for d in range(1, tys):
                back_ty(g, d, ty, tx).start()

        owned(tx, body)

    def spread_ty(g):
        for d in range(1, tiles):
            source = lax.rem(tx - d + tiles, tiles)

            def body():
                back_tile(g, d, source).wait_recv()
                for e in range(1, tys):
                    back_ty(g, e, ty, source).start()

            owned(source, body)

    def finish(g):
        for d in range(1, tys):
            for c in range(owners):
                back_ty(g, d, lax.rem(ty - d + tys, tys), jnp.int32(c)).wait_recv()
        stores[g].start()

    def drain_sums(g):
        for d in range(1, tys):
            for c in range(owners):
                ty_copy(g, d, c).wait_send()
        for d in range(1, tiles):
            owned(lax.rem(tx + d, tiles), lambda: tile_copy(g, d).wait_send())

    def drain_back(g):
        for d in range(1, tys):
            for c in range(owners):
                back_ty(g, d, ty, jnp.int32(c)).wait_send()
        for d in range(1, tiles):
            owned(tx, lambda: back_tile(g, d, tx).wait_send())

    plain = ((1,), (0,))
    across = ((1,), (1,))
    pick_own(inputs.astype(BF), own_a, False)
    loads[3].wait()
    forward_weight(w1, wf1)
    loads[6].wait()
    loads[7].wait()
    wait_halo(0)
    pick_halo(0, halo_a, False)
    first = convolve(own_a, halo_a, wf1, plain) + twice(b1)
    hidden = (first * jax.nn.sigmoid(first)).astype(BF)
    send_halo(1, hidden)
    pick_own(hidden, own_b, False)
    loads[4].wait()
    loads[5].wait()
    forward_weight(w2, wf2)
    turned_weight(w2, wt2)
    upstream = cot[...].astype(F32)
    upstream = jnp.concatenate([upstream, upstream], axis=0).T
    wait_halo(1)
    pick_halo(1, halo_b, False)
    second = convolve(own_b, halo_b, wf2, plain) + twice(b2)
    grad_out = (upstream * silu_slope(inputs + second)).astype(BF)

    send_halo(2, grad_out)
    reduce_start(1, grad_out, buckets[2], own_b, halo_b)
    pick_own(grad_out, own_c, True)
    turned_weight(w1, wt1)
    wait_halo(2)
    pick_halo(2, halo_c, True)
    back = convolve(own_c, halo_c, wt2, across)
    grad_pre = (back * silu_slope(first)).astype(BF)
    send_halo(3, grad_pre)
    reduce_start(0, grad_pre, buckets[3], own_a, halo_a)
    reduce_tiles(1)
    pick_own(grad_pre, own_c, True)
    spread_tiles(1)
    wait_halo(3)
    pick_halo(3, halo_c, True)
    reduce_tiles(0)
    spread_ty(1)
    back = convolve(own_c, halo_c, wt1, across)
    gf[...] = (grad_out.astype(F32) + back).T[:chan]
    stores[2].start()
    spread_tiles(0)
    for stage in range(4):
        wait_sent(stage)
    drain_sums(1)
    spread_ty(0)
    drain_sums(0)
    finish(1)
    drain_back(1)
    finish(0)
    drain_back(0)
    for store in stores:
        store.wait()


def unpack(
    scale, gf_in, full_in, gf_out, gw1_out, gb1_out, gw2_out, gb2_out,
    gf, full, gw, gb1, gb2, in_sem, out_sem,
):
    chan = gf.shape[0]
    loads = [
        pltpu.make_async_copy(full_in.at[g], full.at[g], in_sem.at[g]) for g in range(2)
    ] + [pltpu.make_async_copy(gf_in, gf, in_sem.at[2])]
    for load in loads:
        load.start()
    stores = []

    def store(src, dst):
        copy = pltpu.make_async_copy(src, dst, out_sem.at[len(stores)])
        copy.start()
        stores.append(copy)

    for g, gw_out, gb, gb_out in ((0, gw1_out, gb1, gb1_out), (1, gw2_out, gb2, gb2_out)):
        loads[g].wait()
        for j in range(PAIRS - 2):
            value = full[g, j * chan : (j + 1) * chan, :].astype(F32) * scale
            gw[g, 2 * j] = value[:, :chan]
            if 2 * j + 1 < OFFS:
                gw[g, 2 * j + 1] = value[:, chan:]
            else:
                gb[...] = value[:1, chan:]
        store(gw.at[g], gw_out)
        store(gb, gb_out)
    loads[2].wait()
    store(gf, gf_out.at[0, 0])
    for copy in stores:
        copy.wait()


def per_device(feats, weight1, bias1, weight2, bias2, cotangent, neighbors, shell):
    tiles, chs, subs = (lax.axis_size(a) for a in ("tile", "ch", "sub"))
    chan, vox = feats.shape[2:]
    tys = chs * subs
    scale = 1.0 / math.sqrt(vox * tiles * tys)
    rows = PAIRS * chan
    quarter = rows // tys
    chunk = max(chan, quarter // tiles)
    owners = quarter // chunk
    wide = (PAIRS - 2) * 2 * chan
    lanes = 2 * chan
    edge = 4 * SLOT
    hbm = pl.BlockSpec(memory_space=pltpu.HBM)
    dma = pltpu.SemaphoreType.DMA
    gf, full = pl.pallas_call(
        functools.partial(kernel, tiles, chs, subs),
        out_shape=(
            jax.ShapeDtypeStruct((chan, vox), F32),
            jax.ShapeDtypeStruct((2, rows, lanes), BF),
        ),
        in_specs=[hbm] * 8,
        out_specs=(hbm, hbm),
        scratch_shapes=[
            pltpu.VMEM((chan, vox), BF),
            pltpu.VMEM(weight1.shape, BF),
            pltpu.VMEM((1, chan), F32),
            pltpu.VMEM(weight2.shape, BF),
            pltpu.VMEM((1, chan), F32),
            pltpu.VMEM((chan, vox), BF),
            pltpu.VMEM((OFFS, vox), jnp.int32),
            pltpu.VMEM(shell.shape[2:], jnp.int32),
            dma((8,)),
            pltpu.VMEM((chan, vox), F32),
            dma((3,)),
            pltpu.VMEM(((OFFS + 2) * vox, vox), BF),
            pltpu.VMEM((4, (OFFS + 2) * SLOT, BESIDE * SLOT), BF),
            pltpu.VMEM((4, (len(RING) + 3) * SLOT, lanes), BF),
            pltpu.VMEM((vox, wide), BF),
            pltpu.VMEM((vox, wide), BF),
            pltpu.VMEM((vox, wide), BF),
            pltpu.VMEM((edge, wide), BF),
            pltpu.VMEM((edge, wide), BF),
            pltpu.VMEM((edge, wide), BF),
            pltpu.VMEM((wide, lanes), BF),
            pltpu.VMEM((wide, lanes), BF),
            pltpu.VMEM((lanes, wide), BF),
            pltpu.VMEM((lanes, wide), BF),
            pltpu.VMEM((edge, vox), BF),
            pltpu.VMEM((vox, 2 * edge), BF),
            pltpu.VMEM((4, edge, lanes), BF),
            pltpu.VMEM((vox, 128), F32),
            pltpu.VMEM((2, rows, lanes), BF),
            pltpu.VMEM((2, tys, quarter, lanes), BF),
            pltpu.VMEM((2, quarter, lanes), BF),
            pltpu.VMEM((2, tiles, chunk, lanes), BF),
            pltpu.VMEM((2, rows, lanes), BF),
            dma((4, len(RING))),
            dma((4, len(RING))),
            dma((2, tys, owners)),
            dma((2, tys, owners)),
            dma((2, tiles)),
            dma((2, tiles)),
            dma((2, tiles)),
            dma((2, tiles)),
            dma((2, tys, owners)),
            dma((2, tys, owners)),
        ],
        compiler_params=pltpu.CompilerParams(
            collective_id=0, has_side_effects=True, vmem_limit_bytes=63 * 1024 * 1024
        ),
    )(feats, weight1, bias1[None], weight2, bias2[None], cotangent, neighbors.reshape(OFFS, 1, vox), shell)
    gf, gw1, gb1, gw2, gb2 = pl.pallas_call(
        functools.partial(unpack, scale),
        out_shape=(
            jax.ShapeDtypeStruct((1, 1, chan, vox), F32),
            jax.ShapeDtypeStruct((OFFS, chan, chan), F32),
            jax.ShapeDtypeStruct((1, chan), F32),
            jax.ShapeDtypeStruct((OFFS, chan, chan), F32),
            jax.ShapeDtypeStruct((1, chan), F32),
        ),
        in_specs=[hbm] * 2,
        out_specs=(hbm,) * 5,
        scratch_shapes=[
            pltpu.VMEM((chan, vox), F32),
            pltpu.VMEM((2, rows, lanes), BF),
            pltpu.VMEM((2, OFFS, chan, chan), F32),
            pltpu.VMEM((1, chan), F32),
            pltpu.VMEM((1, chan), F32),
            dma((3,)),
            dma((5,)),
        ],
        compiler_params=pltpu.CompilerParams(vmem_limit_bytes=63 * 1024 * 1024),
    )(gf, full)
    return gf, gw1, gb1[0], gw2, gb2[0]


def solution(mesh):
    placed = (
        P(("parts", "tile"), ("ch", "sub"), None, None),
        P(),
        P(),
        P(),
        P(),
        P(("parts", "tile"), ("ch", "sub"), None, None),
        P(("parts", "tile"), ("ch", "sub"), None, None),
        P(("parts", "tile"), ("ch", "sub"), None, None, None),
    )
    return jax.shard_map(
        per_device,
        mesh=mesh,
        in_specs=placed,
        out_specs=(
            P(("parts", "tile"), ("ch", "sub"), None, None),
            P("parts", None, None),
            P("parts"),
            P("parts", None, None),
            P("parts"),
        ),
        check_vma=False,
    )
```
